32 devices in a mesh: groups: 2 (over y), tensor: 8 (over z, x), dp: 2 (over core).
Axes of the slice: x: 2, y: 2, z: 4, core: 2. Of those that a mesh axis runs over, the one named last changes fastest.
Arguments:
- queries: bfloat16 [1024, 4096], P(('groups', 'dp', 'tensor')), parts along dimension 0, may hold values from -5 to 5
- token_key_rows: bfloat16 [1024, 512], P(('groups', 'dp', 'tensor')), parts along dimension 0, may hold values from -4.5 to 4.5
- token_value_rows: bfloat16 [1024, 512], P(('groups', 'dp', 'tensor')), parts along dimension 0, may hold values from -8 to 8
- stored_key_cache: bfloat16 [1024, 64, 512], P(('groups', 'dp', 'tensor')), parts along dimension 0, may hold values from -4.5 to 4.5
- stored_value_cache: bfloat16 [1024, 64, 512], P(('groups', 'dp', 'tensor')), parts along dimension 0, may hold values from -8 to 8
- cache_position_length: int32 [1024], P(('groups', 'dp', 'tensor')), parts along dimension 0, may hold values from 1 to 64, 16384 in all
- request_adapter_index: int32 [1024, 1], P(('groups', 'dp', 'tensor')), parts along dimension 0, may hold values from 0 to 7; in each aligned block of 32 rows (0 to 31, 32 to 63, ...) at most 4 rows name the same one
- adapter_slot_index: int32 [8], replicated, may hold values from 0 to 7, each once
- output_projection_weight: bfloat16 [4096, 8192], P('tensor'), may hold values from -0.09375 to 0.09375
- down_factor_weight: bfloat16 [8, 4096, 64], P('tensor'), may hold values from -0.09375 to 0.09375
- up_factor_weight: bfloat16 [8, 64, 8192], P('tensor'), may hold values from -0.75 to 0.75
Outputs:
- mixed: bfloat16 [1024, 8192], P(('groups', 'dp', 'tensor')), parts along dimension 0
The draws below stay inside these ranges and needn't reach their ends.
There are 2 independent parts, one for each index of `groups`. The reference program is written for one: setup_inputs(seed, part) draws one part's arguments, and reference() takes and returns one part's arrays. A program takes and returns all parts, laid end to end along the dimension named above; an argument that names none is the same for every part. Nothing has to cross between parts.
Inputs may be any that keep to these rules, and one draw needn't show every extreme that they name: `request_adapter_index`: in the rows of one device (aligned blocks of 32 rows) no adapter is named by more than 4 requests; some block reaches 4. `adapter_slot_index`: A permutation of the adapters over slots; slot s lies on the device of tensor index s. `cache_position_length`: they sum to 16384 in each group; the longest is exactly 64.
All inputs are finite; a program needn't handle non-finite values.
Results may differ from the reference program's by a relative error of at most 0.013.
Values may be sent and summed in bfloat16 or wider, within the bound.
A program may use at most 128 MiB of HBM per device.

```python
import math
import jax
import jax.numpy as jnp
import numpy as np

MODEL_WIDTH = 8192
H = 32
KVH = 4
HD = 128
ADAPTER_RANK = 64
RQ = 32
KV_LEN = 64
QUERY_FEATURES = 4096
MOST = 4
REQ = 512
ADAPTERS_GROUP = 8


def draw_queries(key, part):
    key = jax.random.fold_in(key, 5)
    values = jnp.clip(jax.random.normal(key, (REQ, QUERY_FEATURES), jnp.float32), -4.0, 4.0)
    return values.astype(jnp.bfloat16)


def draw_stored_key_cache(key, part):
    key = jax.random.fold_in(key, 6)
    values = jnp.clip(jax.random.normal(key, (REQ, KV_LEN, KVH * HD), jnp.float32), -4.5, 4.5)
    return values.astype(jnp.bfloat16)


def draw_token_key_rows(key, part):
    key = jax.random.fold_in(key, 7)
    values = jnp.clip(jax.random.normal(key, (REQ, KVH * HD), jnp.float32), -4.5, 4.5)
    return values.astype(jnp.bfloat16)


def block_scale(rng, shape, shards, low, high):
    def one(axis_at, blocks):
        draws = jax.random.uniform(jax.random.fold_in(jax.random.fold_in(rng, 6), axis_at), (blocks,), jnp.float32, low / len(shards), high / len(shards))
        return jnp.repeat(jnp.exp(draws), shape[axis_at] // blocks).reshape((-1,) + (1,) * (len(shape) - axis_at - 1))

    gain = one(*shards[0])
    for cut in shards[1:]:
        gain = gain * one(*cut)
    return gain


def profile(amount, total, most, skew):
    loads = [(1 << 20) // math.isqrt(grade ** skew) + 1 for grade in range(2, amount + 1)]
    spare, given = total - most - (amount - 1), [1] * (amount - 1)
    while spare > 0:
        movable = [i for i in range(amount - 1) if given[i] < most]
        whole, remaining = sum([loads[i] for i in movable]), spare
        for i in movable:
            addition = min(most - given[i], max(1, remaining * loads[i] // whole), spare)
            given[i] = given[i] + addition
            spare = spare - addition
    return np.array([most] + given)


def ragged_sizes(key, count, total, bound, skew):
    if count == 2:
        one = jax.random.randint(key, (), max(1, total - bound), min(bound, total - 1) + 1)
        return jnp.stack([one, total - one])
    sizes = jnp.asarray(profile(count, total, bound, skew), jnp.int32)
    couples = (count - 1) // 2
    donor, receiver = sizes[1:1 + 2 * couples:2], sizes[2:2 + 2 * couples:2]
    room = jnp.minimum(donor - 1, bound - receiver)
    moved = jax.random.randint(jax.random.fold_in(key, 1), (couples,), 0, 1 << 20) % (room + 1)
    sizes = sizes.at[1:1 + 2 * couples:2].set(donor - moved).at[2:2 + 2 * couples:2].set(receiver + moved)
    return sizes[jax.random.permutation(jax.random.fold_in(key, 2), count)]


def deal_out(stream_key, own, number, rows, number_of, top, most, lean):
    ranking = jax.random.permutation(stream_key, number_of)
    heavy_load, usual = load_shares(number_of, rows * top, most, lean, True), load_shares(number_of, rows * top, most, lean, False)
    places = jnp.arange(number_of)

    def named(tallies, rotation):
        used = int((tallies > 0).sum())
        fixed = max(1, used // 4)
        passed = fixed + (places - fixed + rotation * (used - fixed)) % max(1, number_of - fixed)
        return jnp.zeros((number_of,), jnp.int32).at[ranking[jnp.where(places < fixed, places, passed)]].set(jnp.asarray(tallies, jnp.int32))

    tallies = jnp.where(number % 4 == 0, named(heavy_load, number // 4), named(usual, number - number // 4 - 1))
    mixed = jax.random.permutation(jax.random.fold_in(own, 3), number_of)
    donor, taker = mixed[0:number_of // 2 * 2:2], mixed[1:number_of // 2 * 2:2]
    room = jnp.minimum(tallies[donor] - 1, most - tallies[taker]) // 2
    room = jnp.where((donor == ranking[0]) | (taker == ranking[0]) | (tallies[taker] == 0), 0, jnp.maximum(room, 0))
    passed = jax.random.randint(jax.random.fold_in(own, 4), (number_of // 2,), 0, 1 << 20) % (room + 1)
    tallies = tallies.at[donor].add(-passed).at[taker].add(passed)
    items = jnp.searchsorted(jnp.cumsum(tallies), jnp.arange(rows * top), side="right").astype(jnp.int32)
    grid = items.reshape(top, rows).T
    grid = grid[jax.random.permutation(jax.random.fold_in(own, 1), rows)]
    rotation = jax.random.randint(jax.random.fold_in(own, 2), (rows, 1), 0, top)
    return jnp.take_along_axis(grid, (jnp.arange(top)[None, :] + rotation) % top, axis=1)


def load_shares(amount, total, bound, skew, full):
    portions = [(1 << 20) // math.isqrt(rank ** skew) + 1 for rank in range(1, amount + 1)]
    largest = bound if full else min(bound, max(-(-total // amount), total * portions[0] // sum(portions)))
    least = 1 if total - largest >= amount - 1 else 0
    given, spare = [largest] + [least] * (amount - 1), total - largest - least * (amount - 1)
    while spare > 0:
        candidates = [i for i in range(1, amount) if given[i] < largest] or [i for i in range(1, amount) if given[i] < bound]
        whole, budget = sum([portions[i] for i in candidates]), spare
        for i in candidates:
            more = min(bound - given[i], max(1, budget * portions[i] // whole), spare)
            given[i] = given[i] + more
            spare = spare - more
    return np.array(given)


def gaussian(stream_key, shape, width, most, pieces=(), kind=jnp.bfloat16):
    factor_of = block_scale(stream_key, shape, pieces, -0.22, 0.18) if pieces else 1.0
    values = jax.random.normal(stream_key, shape, jnp.float32) * width * factor_of
    return jnp.minimum(jnp.maximum(values, -most), most).astype(kind)


def setup_inputs(seed: int = 0, part: int = 0) -> dict:
    keys = jax.random.split(jax.random.key(seed), 12)
    own_keys = jax.random.split(jax.random.fold_in(keys[11], part), 12)
    queries = draw_queries(jax.random.fold_in(jax.random.fold_in(keys[11], part), 71), part)
    token_key_rows = draw_token_key_rows(jax.random.fold_in(jax.random.fold_in(keys[11], part), 71), part)
    token_value_rows = gaussian(own_keys[2], (REQ, KVH * HD), 2.0, 8.0, ((0, 16),))
    stored_key_cache = draw_stored_key_cache(jax.random.fold_in(jax.random.fold_in(keys[11], part), 71), part)
    stored_value_cache = gaussian(own_keys[4], (REQ, KV_LEN, KVH * HD), 2.0, 8.0, ((0, 16),))
    cache_position_length = ragged_sizes(own_keys[5], REQ, REQ * KV_LEN // 2, KV_LEN, 2).astype(jnp.int32)
    request_adapter_index_keys = jax.random.split(jax.random.fold_in(own_keys[6], 1), REQ // RQ)
    request_adapter_index_turns = jax.random.permutation(jax.random.fold_in(own_keys[6], 3), REQ // RQ)
    request_adapter_index = jax.vmap(lambda own, number: deal_out(jax.random.fold_in(own_keys[6], 2), own, number, RQ, ADAPTERS_GROUP, 1, MOST, 2))(request_adapter_index_keys, request_adapter_index_turns).reshape((REQ, 1))
    adapter_slot_index = jax.random.permutation(keys[7], ADAPTERS_GROUP).astype(jnp.int32)
    output_projection_weight = gaussian(keys[8], (QUERY_FEATURES, MODEL_WIDTH), QUERY_FEATURES ** -0.5, 0.09375, ((0, 8),))
    down_factor_weight = gaussian(keys[9], (ADAPTERS_GROUP, QUERY_FEATURES, ADAPTER_RANK), QUERY_FEATURES ** -0.5, 0.09375, ((0, 8),))
    up_factor_weight = gaussian(keys[10], (ADAPTERS_GROUP, ADAPTER_RANK, MODEL_WIDTH), ADAPTER_RANK ** -0.5, 0.75, ((0, 8),))
    return {"queries": queries, "token_key_rows": token_key_rows, "token_value_rows": token_value_rows, "stored_key_cache": stored_key_cache, "stored_value_cache": stored_value_cache, "cache_position_length": cache_position_length, "request_adapter_index": request_adapter_index, "adapter_slot_index": adapter_slot_index, "output_projection_weight": output_projection_weight, "down_factor_weight": down_factor_weight, "up_factor_weight": up_factor_weight}


def attend(queries, token_key_rows, token_value_rows, stored_key_cache, stored_value_cache, cache_position_length):
    req_count = queries.shape[0]
    per_group = H // KVH
    score_scale = HD ** -0.5
    query_heads = queries.astype(jnp.float32).reshape(req_count, KVH, per_group, HD)
    cached_keys = stored_key_cache.astype(jnp.float32).reshape(req_count, KV_LEN, KVH, HD)
    cached_values = stored_value_cache.astype(jnp.float32).reshape(req_count, KV_LEN, KVH, HD)
    fresh_keys = token_key_rows.astype(jnp.float32).reshape(req_count, KVH, HD)
    fresh_values = token_value_rows.astype(jnp.float32).reshape(req_count, KVH, HD)
    scores = jnp.einsum("rkgd,rlkd->rkgl", query_heads, cached_keys) * score_scale
    fresh = jnp.einsum("rkgd,rkd->rkg", query_heads, fresh_keys) * score_scale
    live = (jnp.arange(KV_LEN, dtype=jnp.int32)[None, :] < cache_position_length[:, None])[:, None, None, :]
    row_top = jnp.maximum(jnp.max(jnp.where(live, scores, -1e30), axis=-1), fresh)
    weights = jnp.where(live, jnp.exp(scores - row_top[..., None]), 0.0)
    fresh_weight = jnp.exp(fresh - row_top)
    total = jnp.sum(weights, axis=-1) + fresh_weight
    probs = (weights / total[..., None]).astype(jnp.bfloat16)
    fresh_prob = (fresh_weight / total).astype(jnp.bfloat16)
    summed = jnp.einsum("rkgl,rlkd->rkgd", probs.astype(jnp.float32), cached_values)
    summed = summed + fresh_prob.astype(jnp.float32)[..., None] * fresh_values[:, :, None, :]
    return summed.reshape(req_count, QUERY_FEATURES).astype(jnp.bfloat16)


def reference(queries, token_key_rows, token_value_rows, stored_key_cache, stored_value_cache, cache_position_length, request_adapter_index, adapter_slot_index, output_projection_weight, down_factor_weight, up_factor_weight):
    attn = attend(queries, token_key_rows, token_value_rows, stored_key_cache, stored_value_cache, cache_position_length)
    base = jnp.dot(attn, output_projection_weight, preferred_element_type=jnp.float32)
    adapter_range = jnp.arange(ADAPTERS_GROUP, dtype=jnp.int32)
    slot = jnp.sum(jnp.where(request_adapter_index == adapter_range[None, :], adapter_slot_index[None, :], 0), axis=1).astype(jnp.int32)
    slot_mask = (slot[:, None] == adapter_range[None, :]).astype(jnp.float32)
    down_factor_rows = jnp.transpose(down_factor_weight, (1, 0, 2)).reshape(QUERY_FEATURES, ADAPTERS_GROUP * ADAPTER_RANK)
    low_all = jnp.dot(attn, down_factor_rows, preferred_element_type=jnp.float32).reshape(-1, ADAPTERS_GROUP, ADAPTER_RANK)
    reduced_rank_rows = jnp.sum(low_all * slot_mask[:, :, None], axis=1).astype(jnp.bfloat16)
    dispersed_rows = (slot_mask.astype(jnp.bfloat16)[:, :, None] * reduced_rank_rows[:, None, :]).reshape(-1, ADAPTERS_GROUP * ADAPTER_RANK)
    adapter_update = jnp.dot(dispersed_rows, up_factor_weight.reshape(ADAPTERS_GROUP * ADAPTER_RANK, MODEL_WIDTH), preferred_element_type=jnp.float32)
    return (base + adapter_update).astype(jnp.bfloat16)
```

```python
import jax
import jax.numpy as jnp
from jax import lax
from jax.sharding import PartitionSpec as P

H = 32
KVH = 4
HD = 128
MOST = 4


def attend(
    queries,
    token_key_rows,
    token_value_rows,
    stored_key_cache,
    stored_value_cache,
    cache_position_length,
):
    req_count = queries.shape[0]
    cache_len = stored_key_cache.shape[1]
    per_group = H // KVH
    score_scale = HD ** (-0.5)
    query_heads = queries.reshape(req_count, KVH, per_group, HD)
    cached_keys = stored_key_cache.reshape(req_count, cache_len, KVH, HD)
    cached_values = stored_value_cache.reshape(req_count, cache_len, KVH, HD)
    fresh_keys = token_key_rows.reshape(req_count, KVH, HD)
    fresh_values = token_value_rows.astype(jnp.float32).reshape(req_count, KVH, HD)
    scores = (
        jnp.einsum("rkgd,rlkd->rkgl", query_heads, cached_keys, preferred_element_type=jnp.float32)
        * score_scale
    )
    fresh = (
        jnp.einsum("rkgd,rkd->rkg", query_heads, fresh_keys, preferred_element_type=jnp.float32)
        * score_scale
    )
    live = (jnp.arange(cache_len, dtype=jnp.int32)[None, :] < cache_position_length[:, None])[
        :, None, None, :
    ]
    row_top = jnp.maximum(jnp.max(jnp.where(live, scores, -1e30), axis=-1), fresh)
    weights = jnp.where(live, jnp.exp(scores - row_top[..., None]), 0.0)
    fresh_weight = jnp.exp(fresh - row_top)
    total = jnp.sum(weights, axis=-1) + fresh_weight
    probs = (weights / total[..., None]).astype(jnp.bfloat16)
    fresh_prob = (fresh_weight / total).astype(jnp.bfloat16)
    summed = jnp.einsum("rkgl,rlkd->rkgd", probs, cached_values, preferred_element_type=jnp.float32)
    summed = summed + fresh_prob.astype(jnp.float32)[..., None] * fresh_values[:, :, None, :]
    return summed.reshape(req_count, KVH * per_group * HD).astype(jnp.bfloat16)


def on_device(
    queries,
    token_key_rows,
    token_value_rows,
    stored_key_cache,
    stored_value_cache,
    cache_position_length,
    request_adapter_index,
    adapter_slot_index,
    output_projection_weight,
    down_factor_weight,
    up_factor_weight,
):
    attn = attend(
        queries,
        token_key_rows,
        token_value_rows,
        stored_key_cache,
        stored_value_cache,
        cache_position_length,
    )
    row_count = attn.shape[0]
    width = attn.shape[1]
    peers = lax.axis_size("tensor")
    heads = lax.all_to_all(attn, "tensor", split_axis=1, concat_axis=0, tiled=True)
    adapter_count = adapter_slot_index.shape[0]
    home = jnp.sum(
        jnp.where(
            request_adapter_index == jnp.arange(adapter_count, dtype=jnp.int32)[None, :],
            adapter_slot_index[None, :],
            0,
        ),
        axis=1,
    )
    positions = jnp.arange(row_count, dtype=jnp.int32)
    same_home = (home[:, None] == home[None, :]) & (positions[:, None] > positions[None, :])
    rank_in_home = jnp.sum(same_home.astype(jnp.int32), axis=1)
    target = home * MOST + rank_in_home
    pick_mask = jnp.arange(peers * MOST, dtype=jnp.int32)[:, None] == target[None, :]
    pick = pick_mask.astype(jnp.bfloat16)
    outgoing = (
        jnp.dot(pick, attn, preferred_element_type=jnp.float32)
        .astype(jnp.bfloat16)
        .reshape(peers, MOST, width)
    )
    numbers = (positions + 1).astype(jnp.float32)
    tags = jnp.dot(pick_mask.astype(jnp.float32), numbers).astype(jnp.bfloat16)
    tags = jnp.broadcast_to(tags.reshape(peers, MOST, 1), (peers, MOST, 128))
    arriving = lax.all_to_all(
        jnp.concatenate([outgoing, tags], axis=2), "tensor", split_axis=0, concat_axis=0, tiled=True
    ).reshape(peers * MOST, width + 128)
    low = jnp.dot(
        arriving[:, :width], down_factor_weight[0], preferred_element_type=jnp.float32
    ).astype(jnp.bfloat16)
    tag_int = arriving[:, width].astype(jnp.int32)
    base_row = (jnp.arange(peers * MOST, dtype=jnp.int32) // MOST) * row_count
    dest = jnp.where(tag_int > 0, base_row + tag_int - 1, -1)[None, :]
    place = (jnp.arange(peers * row_count, dtype=jnp.int32)[:, None] == dest).astype(jnp.bfloat16)
    placed = jnp.dot(place, low, preferred_element_type=jnp.float32).astype(jnp.bfloat16)
    projected = jnp.dot(heads, output_projection_weight, preferred_element_type=jnp.float32)
    delta = jnp.dot(placed, up_factor_weight[0], preferred_element_type=jnp.float32)
    return lax.psum_scatter(
        (projected + delta).astype(jnp.bfloat16), "tensor", scatter_dimension=0, tiled=True
    )


def solution(mesh):
    in_specs = (
        P(("groups", "dp", "tensor"), None),
        P(("groups", "dp", "tensor"), None),
        P(("groups", "dp", "tensor"), None),
        P(("groups", "dp", "tensor"), None, None),
        P(("groups", "dp", "tensor"), None, None),
        P(("groups", "dp", "tensor")),
        P(("groups", "dp", "tensor"), None),
        P(),
        P("tensor", None),
        P("tensor", None, None),
        P("tensor", None, None),
    )
    out_specs = P(("groups", "dp", "tensor"), None)
    return jax.shard_map(
        on_device, mesh=mesh, in_specs=in_specs, out_specs=out_specs, check_vma=False
    )
```

```python
import functools

import jax
import jax.numpy as jnp
from jax import lax
from jax.experimental import pallas as pl
from jax.experimental.pallas import tpu as pltpu
from jax.sharding import PartitionSpec as P

H = 32
KVH = 4
HD = 128
MOST = 4


def attend(
    queries,
    token_key_rows,
    token_value_rows,
    stored_key_cache,
    stored_value_cache,
    cache_position_length,
):
    req_count = queries.shape[0]
    cache_len = stored_key_cache.shape[1]
    per_group = H // KVH
    score_scale = HD ** (-0.5)
    query_heads = queries.reshape(req_count, KVH, per_group, HD)
    cached_keys = stored_key_cache.reshape(req_count, cache_len, KVH, HD)
    cached_values = stored_value_cache.reshape(req_count, cache_len, KVH, HD)
    fresh_keys = token_key_rows.reshape(req_count, KVH, HD)
    fresh_values = token_value_rows.astype(jnp.float32).reshape(req_count, KVH, HD)
    scores = (
        jnp.einsum("rkgd,rlkd->rkgl", query_heads, cached_keys, preferred_element_type=jnp.float32)
        * score_scale
    )
    fresh = (
        jnp.einsum("rkgd,rkd->rkg", query_heads, fresh_keys, preferred_element_type=jnp.float32)
        * score_scale
    )
    live = (jnp.arange(cache_len, dtype=jnp.int32)[None, :] < cache_position_length[:, None])[
        :, None, None, :
    ]
    row_top = jnp.maximum(jnp.max(jnp.where(live, scores, -1e30), axis=-1), fresh)
    weights = jnp.where(live, jnp.exp(scores - row_top[..., None]), 0.0)
    fresh_weight = jnp.exp(fresh - row_top)
    total = jnp.sum(weights, axis=-1) + fresh_weight
    probs = (weights / total[..., None]).astype(jnp.bfloat16)
    fresh_prob = (fresh_weight / total).astype(jnp.bfloat16)
    summed = jnp.einsum("rkgl,rlkd->rkgd", probs, cached_values, preferred_element_type=jnp.float32)
    summed = summed + fresh_prob.astype(jnp.float32)[..., None] * fresh_values[:, :, None, :]
    return summed.reshape(req_count, KVH * per_group * HD).astype(jnp.bfloat16)


CHUNKS = 8


def project_kernel(
    lines,
    lhs_ref,
    weight_ref,
    up_ref,
    out_ref,
    weights,
    pair_out,
    pair_in,
    line_out,
    line_in,
    own,
    kept,
    weight_sem,
    up_sem,
    pair_send,
    pair_recv,
    line_send,
    line_recv,
):
    me = lax.axis_index("tensor")
    line, side = me // 2, me % 2
    other = 2 * line + (1 - side)
    depth = weight_ref.shape[0]
    rank = up_ref.shape[0]
    rows = lhs_ref.shape[2]
    span = pair_out.shape[3]

    def columns(c):
        return pl.ds(pl.multiple_of(c * span, span), span)

    def weight_copy(c):
        return pltpu.make_async_copy(
            weight_ref.at[:, columns(c)], weights.at[c, pl.ds(0, depth)], weight_sem.at[c]
        )

    def up_copy(c):
        return pltpu.make_async_copy(
            up_ref.at[:, columns(c)], weights.at[c, pl.ds(depth, rank)], up_sem.at[c]
        )

    def pair_copy(c):
        return pltpu.make_async_remote_copy(
            src_ref=pair_out.at[c],
            dst_ref=pair_in.at[c],
            send_sem=pair_send.at[c],
            recv_sem=pair_recv.at[c],
            device_id={"tensor": other},
            device_id_type=pl.DeviceIdType.MESH,
        )

    def line_copy(c, k):
        to = (line + k) % lines
        return pltpu.make_async_remote_copy(
            src_ref=line_out.at[c, k],
            dst_ref=line_in.at[c, k - 1],
            send_sem=line_send.at[c, k - 1],
            recv_sem=line_recv.at[c, k - 1],
            device_id={"tensor": 2 * to + side},
            device_id_type=pl.DeviceIdType.MESH,
        )

    @pl.loop(0, CHUNKS)
    def _(c):
        weight_copy(c).start()
        up_copy(c).start()

    barrier = pltpu.get_barrier_semaphore()
    pl.semaphore_signal(
        barrier, inc=1, device_id={"tensor": other}, device_id_type=pl.DeviceIdType.MESH
    )
    for k in range(1, lines):
        pl.semaphore_signal(
            barrier,
            inc=1,
            device_id={"tensor": 2 * ((line + k) % lines) + side},
            device_id_type=pl.DeviceIdType.MESH,
        )
    pl.semaphore_wait(barrier, lines)

    @pl.loop(0, CHUNKS)
    def _(c):
        weight_copy(c).wait()
        up_copy(c).wait()
        left = lhs_ref[:, 1 - side].reshape(lines * rows, depth + rank)
        part = jnp.dot(left, weights[c], preferred_element_type=jnp.float32)
        pair_out[c] = part.astype(jnp.bfloat16).reshape(lines, rows, span)
        pair_copy(c).start()

    @pl.loop(0, CHUNKS)
    def _(c):
        left = lhs_ref[:, side].reshape(lines * rows, depth + rank)
        part = jnp.dot(left, weights[c], preferred_element_type=jnp.float32)
        pair_own = part.reshape(lines, rows, span)
        own[...] = pair_own
        pair_copy(c).wait_recv()
        for k in range(lines):
            to = (line + k) % lines
            both = own[to] + pair_in[c, to].astype(jnp.float32)
            if k == 0:
                kept[c] = both
            else:
                line_out[c, k] = both.astype(jnp.bfloat16)
                line_copy(c, k).start()

    @pl.loop(0, CHUNKS)
    def _(c):
        total = kept[c]
        for k in range(1, lines):
            line_copy(c, k).wait_recv()
            total = total + line_in[c, k - 1].astype(jnp.float32)
        out_ref[:, columns(c)] = total.astype(jnp.bfloat16)

    @pl.loop(0, CHUNKS)
    def _(c):
        pair_copy(c).wait_send()
        for k in range(1, lines):
            line_copy(c, k).wait_send()


def project_and_sum(lhs, weight, up, peers):
    lines = peers // 2
    rows = lhs.shape[0] // peers
    depth, width = weight.shape
    rank = up.shape[0]
    span = width // CHUNKS
    dma = pltpu.SemaphoreType.DMA
    return pl.pallas_call(
        functools.partial(project_kernel, lines),
        out_shape=jax.ShapeDtypeStruct((rows, width), jnp.bfloat16),
        in_specs=[
            pl.BlockSpec(memory_space=pltpu.VMEM),
            pl.BlockSpec(memory_space=pl.ANY),
            pl.BlockSpec(memory_space=pl.ANY),
        ],
        out_specs=pl.BlockSpec(memory_space=pltpu.VMEM),
        scratch_shapes=[
            pltpu.VMEM((CHUNKS, depth + rank, span), jnp.bfloat16),
            pltpu.VMEM((CHUNKS, lines, rows, span), jnp.bfloat16),
            pltpu.VMEM((CHUNKS, lines, rows, span), jnp.bfloat16),
            pltpu.VMEM((CHUNKS, lines, rows, span), jnp.bfloat16),
            pltpu.VMEM((CHUNKS, lines - 1, rows, span), jnp.bfloat16),
            pltpu.VMEM((lines, rows, span), jnp.float32),
            pltpu.VMEM((CHUNKS, rows, span), jnp.float32),
            dma((CHUNKS,)),
            dma((CHUNKS,)),
            dma((CHUNKS,)),
            dma((CHUNKS,)),
            dma((CHUNKS, lines - 1)),
            dma((CHUNKS, lines - 1)),
        ],
        compiler_params=pltpu.CompilerParams(
            collective_id=0, has_side_effects=True, vmem_limit_bytes=40 * 1024 * 1024
        ),
        cost_estimate=pl.CostEstimate(
            flops=2 * lhs.shape[0] * (depth + rank) * width,
            bytes_accessed=2 * (depth + rank) * width,
            transcendentals=0,
        ),
    )(lhs.reshape(lines, 2, rows, depth + rank), weight, up)


def on_device(
    queries,
    token_key_rows,
    token_value_rows,
    stored_key_cache,
    stored_value_cache,
    cache_position_length,
    request_adapter_index,
    adapter_slot_index,
    output_projection_weight,
    down_factor_weight,
    up_factor_weight,
):
    attn = attend(
        queries,
        token_key_rows,
        token_value_rows,
        stored_key_cache,
        stored_value_cache,
        cache_position_length,
    )
    row_count = attn.shape[0]
    width = attn.shape[1]
    peers = lax.axis_size("tensor")
    heads = lax.all_to_all(attn, "tensor", split_axis=1, concat_axis=0, tiled=True)
    adapter_count = adapter_slot_index.shape[0]
    home = jnp.sum(
        jnp.where(
            request_adapter_index == jnp.arange(adapter_count, dtype=jnp.int32)[None, :],
            adapter_slot_index[None, :],
            0,
        ),
        axis=1,
    )
    positions = jnp.arange(row_count, dtype=jnp.int32)
    same_home = (home[:, None] == home[None, :]) & (positions[:, None] > positions[None, :])
    rank_in_home = jnp.sum(same_home.astype(jnp.int32), axis=1)
    target = home * MOST + rank_in_home
    pick_mask = jnp.arange(peers * MOST, dtype=jnp.int32)[:, None] == target[None, :]
    pick = pick_mask.astype(jnp.bfloat16)
    outgoing = (
        jnp.dot(pick, attn, preferred_element_type=jnp.float32)
        .astype(jnp.bfloat16)
        .reshape(peers, MOST, width)
    )
    numbers = (positions + 1).astype(jnp.float32)
    tags = jnp.dot(pick_mask.astype(jnp.float32), numbers).astype(jnp.bfloat16)
    tags = jnp.broadcast_to(tags.reshape(peers, MOST, 1), (peers, MOST, 128))
    arriving = lax.all_to_all(
        jnp.concatenate([outgoing, tags], axis=2), "tensor", split_axis=0, concat_axis=0, tiled=True
    ).reshape(peers * MOST, width + 128)
    low = jnp.dot(
        arriving[:, :width], down_factor_weight[0], preferred_element_type=jnp.float32
    ).astype(jnp.bfloat16)
    tag_int = arriving[:, width].astype(jnp.int32)
    base_row = (jnp.arange(peers * MOST, dtype=jnp.int32) // MOST) * row_count
    dest = jnp.where(tag_int > 0, base_row + tag_int - 1, -1)[None, :]
    place = (jnp.arange(peers * row_count, dtype=jnp.int32)[:, None] == dest).astype(jnp.bfloat16)
    placed = jnp.dot(place, low, preferred_element_type=jnp.float32).astype(jnp.bfloat16)
    lhs = jnp.concatenate([heads, placed], axis=1)
    return project_and_sum(lhs, output_projection_weight, up_factor_weight[0], peers)


def solution(mesh):
    in_specs = (
        P(("groups", "dp", "tensor"), None),
        P(("groups", "dp", "tensor"), None),
        P(("groups", "dp", "tensor"), None),
        P(("groups", "dp", "tensor"), None, None),
        P(("groups", "dp", "tensor"), None, None),
        P(("groups", "dp", "tensor")),
        P(("groups", "dp", "tensor"), None),
        P(),
        P("tensor", None),
        P("tensor", None, None),
        P("tensor", None, None),
    )
    out_specs = P(("groups", "dp", "tensor"), None)
    return jax.shard_map(
        on_device, mesh=mesh, in_specs=in_specs, out_specs=out_specs, check_vma=False
    )
```

```python
import functools

import jax
import jax.numpy as jnp
from jax import lax
from jax.experimental import pallas as pl
from jax.experimental.pallas import tpu as pltpu
from jax.sharding import PartitionSpec as P

H = 32
KVH = 4
HD = 128
MOST = 4


def attend(
    queries,
    token_key_rows,
    token_value_rows,
    stored_key_cache,
    stored_value_cache,
    cache_position_length,
):
    req_count = queries.shape[0]
    cache_len = stored_key_cache.shape[1]
    per_group = H // KVH
    score_scale = HD ** (-0.5)
    query_heads = queries.reshape(req_count, KVH, per_group, HD)
    cached_keys = stored_key_cache.reshape(req_count, cache_len, KVH, HD)
    cached_values = stored_value_cache.reshape(req_count, cache_len, KVH, HD)
    fresh_keys = token_key_rows.reshape(req_count, KVH, HD)
    fresh_values = token_value_rows.astype(jnp.float32).reshape(req_count, KVH, HD)
    scores = (
        jnp.einsum("rkgd,rlkd->rkgl", query_heads, cached_keys, preferred_element_type=jnp.float32)
        * score_scale
    )
    fresh = (
        jnp.einsum("rkgd,rkd->rkg", query_heads, fresh_keys, preferred_element_type=jnp.float32)
        * score_scale
    )
    live = (jnp.arange(cache_len, dtype=jnp.int32)[None, :] < cache_position_length[:, None])[
        :, None, None, :
    ]
    row_top = jnp.maximum(jnp.max(jnp.where(live, scores, -1e30), axis=-1), fresh)
    weights = jnp.where(live, jnp.exp(scores - row_top[..., None]), 0.0)
    fresh_weight = jnp.exp(fresh - row_top)
    total = jnp.sum(weights, axis=-1) + fresh_weight
    probs = (weights / total[..., None]).astype(jnp.bfloat16)
    fresh_prob = (fresh_weight / total).astype(jnp.bfloat16)
    summed = jnp.einsum("rkgl,rlkd->rkgd", probs, cached_values, preferred_element_type=jnp.float32)
    summed = summed + fresh_prob.astype(jnp.float32)[..., None] * fresh_values[:, :, None, :]
    return summed.reshape(req_count, KVH * per_group * HD).astype(jnp.bfloat16)


CHUNKS = 8


def project_kernel(
    lines,
    attn_ref,
    target_row_ref,
    target_column_ref,
    down_ref,
    weight_ref,
    up_ref,
    out_ref,
    outbox,
    inbox,
    lhs_ref,
    weights,
    pair_out,
    pair_in,
    line_out,
    line_in,
    own,
    kept,
    mail_send,
    mail_recv,
    weight_sem,
    up_sem,
    pair_send,
    pair_recv,
    line_send,
    line_recv,
):
    me = lax.axis_index("tensor")
    line, side = me // 2, me % 2
    other = 2 * line + (1 - side)
    depth = weight_ref.shape[0]
    rank = up_ref.shape[0]
    rows = lhs_ref.shape[2]
    span = pair_out.shape[3]
    peers = 2 * lines
    blocks = rows // MOST
    block = attn_ref.shape[1] // blocks

    def columns(c):
        return pl.ds(pl.multiple_of(c * span, span), span)

    def weight_copy(c):
        return pltpu.make_async_copy(
            weight_ref.at[:, columns(c)], weights.at[c, pl.ds(0, depth)], weight_sem.at[c]
        )

    def up_copy(c):
        return pltpu.make_async_copy(
            up_ref.at[:, columns(c)], weights.at[c, pl.ds(depth, rank)], up_sem.at[c]
        )

    def mail_copy(k):
        to = (me + k) % peers
        return pltpu.make_async_remote_copy(
            src_ref=outbox.at[to],
            dst_ref=inbox.at[me],
            send_sem=mail_send.at[k - 1],
            recv_sem=mail_recv.at[k - 1],
            device_id={"tensor": to},
            device_id_type=pl.DeviceIdType.MESH,
        )

    def pair_copy(c):
        return pltpu.make_async_remote_copy(
            src_ref=pair_out.at[c],
            dst_ref=pair_in.at[c],
            send_sem=pair_send.at[c],
            recv_sem=pair_recv.at[c],
            device_id={"tensor": other},
            device_id_type=pl.DeviceIdType.MESH,
        )

    def line_copy(c, k):
        to = (line + k) % lines
        return pltpu.make_async_remote_copy(
            src_ref=line_out.at[c, k],
            dst_ref=line_in.at[c, k - 1],
            send_sem=line_send.at[c, k - 1],
            recv_sem=line_recv.at[c, k - 1],
            device_id={"tensor": 2 * to + side},
            device_id_type=pl.DeviceIdType.MESH,
        )

    @pl.loop(0, CHUNKS)
    def _(c):
        weight_copy(c).start()
        up_copy(c).start()

    barrier = pltpu.get_barrier_semaphore()
    for k in range(1, peers):
        pl.semaphore_signal(
            barrier,
            inc=1,
            device_id={"tensor": (me + k) % peers},
            device_id_type=pl.DeviceIdType.MESH,
        )

    for p in range(peers):
        outbox[p, :, :depth] = attn_ref[:, p * depth : (p + 1) * depth]
    picked_shape = (peers * rows, rows)
    spot = lax.broadcasted_iota(jnp.int32, picked_shape, 0)
    wanted = (spot // rows) * MOST + (spot % rows) // blocks
    match = wanted == jnp.broadcast_to(target_row_ref[...], picked_shape)
    picked = jnp.zeros((peers * rows, block), jnp.float32)
    for b in range(blocks):
        pick = jnp.where(match & (spot % blocks == b), 1.0, 0.0).astype(jnp.bfloat16)
        picked = picked + jnp.dot(
            pick,
            attn_ref[:, b * block : (b + 1) * block],
            preferred_element_type=jnp.float32,
        )
    outbox[:, :, depth : depth + block] = picked.astype(jnp.bfloat16).reshape(peers, rows, block)
    target = jnp.broadcast_to(target_column_ref[...], (rows, 128))
    lane = lax.broadcasted_iota(jnp.int32, (rows, 128), 1)
    for p in range(peers):
        here = (target // MOST == p) & (lane == me * MOST + target % MOST)
        outbox[p, :, depth + block :] = jnp.where(here, 1.0, 0.0).astype(jnp.bfloat16)
    pl.semaphore_wait(barrier, peers - 1)
    for k in range(1, peers):
        mail_copy(k).start()
    inbox[me] = outbox[me]
    for k in range(1, peers):
        mail_copy(k).wait_recv()

    arrived = inbox[:, :, depth : depth + block].reshape(peers * rows, block)
    spot = lax.broadcasted_iota(jnp.int32, (peers * rows, rank), 0)
    low = jnp.zeros((peers * rows, rank), jnp.float32)
    for b in range(blocks):
        term = lax.dot_general(
            arrived,
            down_ref[:, b * block : (b + 1) * block],
            (((1,), (1,)), ((), ())),
            preferred_element_type=jnp.float32,
        )
        low = low + jnp.where(spot % blocks == b, term, 0.0)
    low = jnp.sum(low.reshape(peers * MOST, blocks, rank), axis=1)
    low = jnp.concatenate([low, jnp.zeros((128 - peers * MOST, rank), jnp.float32)], axis=0)
    place = inbox[:, :, depth + block :].reshape(peers * rows, 128)
    placed = jnp.dot(place, low.astype(jnp.bfloat16), preferred_element_type=jnp.float32)
    placed = placed.astype(jnp.bfloat16).reshape(lines, 2, rows, rank)
    lhs_ref[:, :, :, :depth] = inbox[:, :, :depth].reshape(lines, 2, rows, depth)
    lhs_ref[:, :, :, depth:] = placed

    @pl.loop(0, CHUNKS)
    def _(c):
        weight_copy(c).wait()
        up_copy(c).wait()
        left = lhs_ref[:, 1 - side].reshape(lines * rows, depth + rank)
        part = jnp.dot(left, weights[c], preferred_element_type=jnp.float32)
        pair_out[c] = part.astype(jnp.bfloat16).reshape(lines, rows, span)
        pair_copy(c).start()

    @pl.loop(0, CHUNKS)
    def _(c):
        left = lhs_ref[:, side].reshape(lines * rows, depth + rank)
        part = jnp.dot(left, weights[c], preferred_element_type=jnp.float32)
        pair_own = part.reshape(lines, rows, span)
        own[...] = pair_own
        pair_copy(c).wait_recv()
        for k in range(lines):
            to = (line + k) % lines
            both = own[to] + pair_in[c, to].astype(jnp.float32)
            if k == 0:
                kept[c] = both
            else:
                line_out[c, k] = both.astype(jnp.bfloat16)
                line_copy(c, k).start()

    @pl.loop(0, CHUNKS)
    def _(c):
        total = kept[c]
        for k in range(1, lines):
            line_copy(c, k).wait_recv()
            total = total + line_in[c, k - 1].astype(jnp.float32)
        out_ref[:, columns(c)] = total.astype(jnp.bfloat16)

    @pl.loop(0, CHUNKS)
    def _(c):
        pair_copy(c).wait_send()
        for k in range(1, lines):
            line_copy(c, k).wait_send()

    for k in range(1, peers):
        mail_copy(k).wait_send()


def project_and_sum(attn, target, down, weight, up, peers):
    lines = peers // 2
    rows = attn.shape[0]
    depth, width = weight.shape
    rank = up.shape[0]
    span = width // CHUNKS
    letter = depth + MOST * attn.shape[1] // rows + 128
    dma = pltpu.SemaphoreType.DMA
    return pl.pallas_call(
        functools.partial(project_kernel, lines),
        out_shape=jax.ShapeDtypeStruct((rows, width), jnp.bfloat16),
        in_specs=[
            pl.BlockSpec(memory_space=pltpu.VMEM),
            pl.BlockSpec(memory_space=pltpu.VMEM),
            pl.BlockSpec(memory_space=pltpu.VMEM),
            pl.BlockSpec(memory_space=pltpu.VMEM),
            pl.BlockSpec(memory_space=pl.ANY),
            pl.BlockSpec(memory_space=pl.ANY),
        ],
        out_specs=pl.BlockSpec(memory_space=pltpu.VMEM),
        scratch_shapes=[
            pltpu.VMEM((peers, rows, letter), jnp.bfloat16),
            pltpu.VMEM((peers, rows, letter), jnp.bfloat16),
            pltpu.VMEM((lines, 2, rows, depth + rank), jnp.bfloat16),
            pltpu.VMEM((CHUNKS, depth + rank, span), jnp.bfloat16),
            pltpu.VMEM((CHUNKS, lines, rows, span), jnp.bfloat16),
            pltpu.VMEM((CHUNKS, lines, rows, span), jnp.bfloat16),
            pltpu.VMEM((CHUNKS, lines, rows, span), jnp.bfloat16),
            pltpu.VMEM((CHUNKS, lines - 1, rows, span), jnp.bfloat16),
            pltpu.VMEM((lines, rows, span), jnp.float32),
            pltpu.VMEM((CHUNKS, rows, span), jnp.float32),
            dma((peers - 1,)),
            dma((peers - 1,)),
            dma((CHUNKS,)),
            dma((CHUNKS,)),
            dma((CHUNKS,)),
            dma((CHUNKS,)),
            dma((CHUNKS, lines - 1)),
            dma((CHUNKS, lines - 1)),
        ],
        compiler_params=pltpu.CompilerParams(
            collective_id=0, has_side_effects=True, vmem_limit_bytes=40 * 1024 * 1024
        ),
        cost_estimate=pl.CostEstimate(
            flops=2 * peers * rows * (depth + rank) * width,
            bytes_accessed=2 * (depth + rank) * width,
            transcendentals=0,
        ),
    )(attn, target.reshape(1, rows), target.reshape(rows, 1), down.T, weight, up)


def on_device(
    queries,
    token_key_rows,
    token_value_rows,
    stored_key_cache,
    stored_value_cache,
    cache_position_length,
    request_adapter_index,
    adapter_slot_index,
    output_projection_weight,
    down_factor_weight,
    up_factor_weight,
):
    attn = attend(
        queries,
        token_key_rows,
        token_value_rows,
        stored_key_cache,
        stored_value_cache,
        cache_position_length,
    )
    row_count = attn.shape[0]
    peers = lax.axis_size("tensor")
    adapter_count = adapter_slot_index.shape[0]
    home = jnp.sum(
        jnp.where(
            request_adapter_index == jnp.arange(adapter_count, dtype=jnp.int32)[None, :],
            adapter_slot_index[None, :],
            0,
        ),
        axis=1,
    )
    positions = jnp.arange(row_count, dtype=jnp.int32)
    same_home = (home[:, None] == home[None, :]) & (positions[:, None] > positions[None, :])
    rank_in_home = jnp.sum(same_home.astype(jnp.int32), axis=1)
    target = home * MOST + rank_in_home
    return project_and_sum(
        attn,
        target,
        down_factor_weight[0],
        output_projection_weight,
        up_factor_weight[0],
        peers,
    )


def solution(mesh):
    in_specs = (
        P(("groups", "dp", "tensor"), None),
        P(("groups", "dp", "tensor"), None),
        P(("groups", "dp", "tensor"), None),
        P(("groups", "dp", "tensor"), None, None),
        P(("groups", "dp", "tensor"), None, None),
        P(("groups", "dp", "tensor")),
        P(("groups", "dp", "tensor"), None),
        P(),
        P("tensor", None),
        P("tensor", None, None),
        P("tensor", None, None),
    )
    out_specs = P(("groups", "dp", "tensor"), None)
    return jax.shard_map(
        on_device, mesh=mesh, in_specs=in_specs, out_specs=out_specs, check_vma=False
    )
```

```python
import functools

import jax
import jax.numpy as jnp
from jax import lax
from jax.experimental import pallas as pl
from jax.experimental.pallas import tpu as pltpu
from jax.sharding import PartitionSpec as P

H = 32
KVH = 4
HD = 128
MOST = 4


def attend(
    queries,
    token_key_rows,
    token_value_rows,
    stored_key_cache,
    stored_value_cache,
    cache_position_length,
):
    req_count = queries.shape[0]
    cache_len = stored_key_cache.shape[1]
    per_group = H // KVH
    score_scale = HD ** (-0.5)
    query_heads = queries.reshape(req_count, KVH, per_group, HD)
    cached_keys = stored_key_cache.reshape(req_count, cache_len, KVH, HD)
    cached_values = stored_value_cache.reshape(req_count, cache_len, KVH, HD)
    fresh_keys = token_key_rows.reshape(req_count, KVH, HD)
    fresh_values = token_value_rows.astype(jnp.float32).reshape(req_count, KVH, HD)
    scores = (
        jnp.einsum("rkgd,rlkd->rkgl", query_heads, cached_keys, preferred_element_type=jnp.float32)
        * score_scale
    )
    fresh = (
        jnp.einsum("rkgd,rkd->rkg", query_heads, fresh_keys, preferred_element_type=jnp.float32)
        * score_scale
    )
    live = (jnp.arange(cache_len, dtype=jnp.int32)[None, :] < cache_position_length[:, None])[
        :, None, None, :
    ]
    row_top = jnp.maximum(jnp.max(jnp.where(live, scores, -1e30), axis=-1), fresh)
    weights = jnp.where(live, jnp.exp(scores - row_top[..., None]), 0.0)
    fresh_weight = jnp.exp(fresh - row_top)
    total = jnp.sum(weights, axis=-1) + fresh_weight
    probs = (weights / total[..., None]).astype(jnp.bfloat16)
    fresh_prob = (fresh_weight / total).astype(jnp.bfloat16)
    summed = jnp.einsum("rkgl,rlkd->rkgd", probs, cached_values, preferred_element_type=jnp.float32)
    summed = summed + fresh_prob.astype(jnp.float32)[..., None] * fresh_values[:, :, None, :]
    return summed.reshape(req_count, KVH * per_group * HD).astype(jnp.bfloat16)


CHUNKS = 16


def project_kernel(
    lines,
    attn_ref,
    target_row_ref,
    target_column_ref,
    down_ref,
    weight_ref,
    up_ref,
    out_ref,
    outbox,
    inbox,
    lhs_ref,
    weights,
    pair_out,
    pair_in,
    line_out,
    line_in,
    own,
    kept,
    mail_send,
    mail_recv,
    weight_sem,
    up_sem,
    pair_send,
    pair_recv,
    line_send,
    line_recv,
):
    me = lax.axis_index("tensor")
    line, side = me // 2, me % 2
    other = 2 * line + (1 - side)
    depth = weight_ref.shape[0]
    rank = up_ref.shape[0]
    rows = lhs_ref.shape[2]
    span = pair_out.shape[3]
    peers = 2 * lines
    blocks = rows // MOST
    block = attn_ref.shape[1] // blocks

    def columns(c):
        return pl.ds(pl.multiple_of(c * span, span), span)

    def weight_copy(c):
        return pltpu.make_async_copy(
            weight_ref.at[:, columns(c)], weights.at[c, pl.ds(0, depth)], weight_sem.at[c]
        )

    def up_copy(c):
        return pltpu.make_async_copy(
            up_ref.at[:, columns(c)], weights.at[c, pl.ds(depth, rank)], up_sem.at[c]
        )

    def mail_copy(k):
        to = (me + k) % peers
        return pltpu.make_async_remote_copy(
            src_ref=outbox.at[to],
            dst_ref=inbox.at[me],
            send_sem=mail_send.at[k - 1],
            recv_sem=mail_recv.at[k - 1],
            device_id={"tensor": to},
            device_id_type=pl.DeviceIdType.MESH,
        )

    def pair_copy(c):
        return pltpu.make_async_remote_copy(
            src_ref=pair_out.at[c],
            dst_ref=pair_in.at[c],
            send_sem=pair_send.at[c],
            recv_sem=pair_recv.at[c],
            device_id={"tensor": other},
            device_id_type=pl.DeviceIdType.MESH,
        )

    def line_copy(c, k):
        to = (line + k) % lines
        return pltpu.make_async_remote_copy(
            src_ref=line_out.at[c, k],
            dst_ref=line_in.at[c, k - 1],
            send_sem=line_send.at[c, k - 1],
            recv_sem=line_recv.at[c, k - 1],
            device_id={"tensor": 2 * to + side},
            device_id_type=pl.DeviceIdType.MESH,
        )

    @pl.loop(0, CHUNKS)
    def _(c):
        weight_copy(c).start()
        up_copy(c).start()

    barrier = pltpu.get_barrier_semaphore()
    for k in range(1, peers):
        pl.semaphore_signal(
            barrier,
            inc=1,
            device_id={"tensor": (me + k) % peers},
            device_id_type=pl.DeviceIdType.MESH,
        )

    for p in range(peers):
        outbox[p, :, :depth] = attn_ref[:, p * depth : (p + 1) * depth]
    picked_shape = (peers * rows, rows)
    spot = lax.broadcasted_iota(jnp.int32, picked_shape, 0)
    wanted = (spot // rows) * MOST + (spot % rows) // blocks
    match = wanted == jnp.broadcast_to(target_row_ref[...], picked_shape)
    picked = jnp.zeros((peers * rows, block), jnp.float32)
    for b in range(blocks):
        pick = jnp.where(match & (spot % blocks == b), 1.0, 0.0).astype(jnp.bfloat16)
        picked = picked + jnp.dot(
            pick,
            attn_ref[:, b * block : (b + 1) * block],
            preferred_element_type=jnp.float32,
        )
    outbox[:, :, depth : depth + block] = picked.astype(jnp.bfloat16).reshape(peers, rows, block)
    target = jnp.broadcast_to(target_column_ref[...], (rows, 128))
    lane = lax.broadcasted_iota(jnp.int32, (rows, 128), 1)
    for p in range(peers):
        here = (target // MOST == p) & (lane == me * MOST + target % MOST)
        outbox[p, :, depth + block :] = jnp.where(here, 1.0, 0.0).astype(jnp.bfloat16)
    pl.semaphore_wait(barrier, peers - 1)
    for k in range(1, peers):
        mail_copy(k).start()
    inbox[me] = outbox[me]
    for k in range(1, peers):
        mail_copy(k).wait_recv()

    arrived = inbox[:, :, depth : depth + block].reshape(peers * rows, block)
    spot = lax.broadcasted_iota(jnp.int32, (peers * rows, rank), 0)
    low = jnp.zeros((peers * rows, rank), jnp.float32)
    for b in range(blocks):
        term = lax.dot_general(
            arrived,
            down_ref[:, b * block : (b + 1) * block],
            (((1,), (1,)), ((), ())),
            preferred_element_type=jnp.float32,
        )
        low = low + jnp.where(spot % blocks == b, term, 0.0)
    low = jnp.sum(low.reshape(peers * MOST, blocks, rank), axis=1)
    low = jnp.concatenate([low, jnp.zeros((128 - peers * MOST, rank), jnp.float32)], axis=0)
    place = inbox[:, :, depth + block :].reshape(peers * rows, 128)
    placed = jnp.dot(place, low.astype(jnp.bfloat16), preferred_element_type=jnp.float32)
    placed = placed.astype(jnp.bfloat16).reshape(lines, 2, rows, rank)
    lhs_ref[:, :, :, :depth] = inbox[:, :, :depth].reshape(lines, 2, rows, depth)
    lhs_ref[:, :, :, depth:] = placed

    @pl.loop(0, CHUNKS)
    def _(c):
        weight_copy(c).wait()
        up_copy(c).wait()
        left = lhs_ref[:, 1 - side].reshape(lines * rows, depth + rank)
        part = jnp.dot(left, weights[c], preferred_element_type=jnp.float32)
        pair_out[c] = part.astype(jnp.bfloat16).reshape(lines, rows, span)
        pair_copy(c).start()

    @pl.loop(0, CHUNKS)
    def _(c):
        left = lhs_ref[:, side].reshape(lines * rows, depth + rank)
        part = jnp.dot(left, weights[c], preferred_element_type=jnp.float32)
        pair_own = part.reshape(lines, rows, span)
        own[...] = pair_own
        pair_copy(c).wait_recv()
        for k in range(lines):
            to = (line + k) % lines
            both = own[to] + pair_in[c, to].astype(jnp.float32)
            if k == 0:
                kept[c] = both
            else:
                line_out[c, k] = both.astype(jnp.bfloat16)
                line_copy(c, k).start()

    @pl.loop(0, CHUNKS)
    def _(c):
        total = kept[c]
        for k in range(1, lines):
            line_copy(c, k).wait_recv()
            total = total + line_in[c, k - 1].astype(jnp.float32)
        out_ref[:, columns(c)] = total.astype(jnp.bfloat16)

    @pl.loop(0, CHUNKS)
    def _(c):
        pair_copy(c).wait_send()
        for k in range(1, lines):
            line_copy(c, k).wait_send()

    for k in range(1, peers):
        mail_copy(k).wait_send()


def project_and_sum(attn, target, down, weight, up, peers):
    lines = peers // 2
    rows = attn.shape[0]
    depth, width = weight.shape
    rank = up.shape[0]
    span = width // CHUNKS
    letter = depth + MOST * attn.shape[1] // rows + 128
    dma = pltpu.SemaphoreType.DMA
    return pl.pallas_call(
        functools.partial(project_kernel, lines),
        out_shape=jax.ShapeDtypeStruct((rows, width), jnp.bfloat16),
        in_specs=[
            pl.BlockSpec(memory_space=pltpu.VMEM),
            pl.BlockSpec(memory_space=pltpu.VMEM),
            pl.BlockSpec(memory_space=pltpu.VMEM),
            pl.BlockSpec(memory_space=pltpu.VMEM),
            pl.BlockSpec(memory_space=pl.ANY),
            pl.BlockSpec(memory_space=pl.ANY),
        ],
        out_specs=pl.BlockSpec(memory_space=pltpu.VMEM),
        scratch_shapes=[
            pltpu.VMEM((peers, rows, letter), jnp.bfloat16),
            pltpu.VMEM((peers, rows, letter), jnp.bfloat16),
            pltpu.VMEM((lines, 2, rows, depth + rank), jnp.bfloat16),
            pltpu.VMEM((CHUNKS, depth + rank, span), jnp.bfloat16),
            pltpu.VMEM((CHUNKS, lines, rows, span), jnp.bfloat16),
            pltpu.VMEM((CHUNKS, lines, rows, span), jnp.bfloat16),
            pltpu.VMEM((CHUNKS, lines, rows, span), jnp.bfloat16),
            pltpu.VMEM((CHUNKS, lines - 1, rows, span), jnp.bfloat16),
            pltpu.VMEM((lines, rows, span), jnp.float32),
            pltpu.VMEM((CHUNKS, rows, span), jnp.float32),
            dma((peers - 1,)),
            dma((peers - 1,)),
            dma((CHUNKS,)),
            dma((CHUNKS,)),
            dma((CHUNKS,)),
            dma((CHUNKS,)),
            dma((CHUNKS, lines - 1)),
            dma((CHUNKS, lines - 1)),
        ],
        compiler_params=pltpu.CompilerParams(
            collective_id=0, has_side_effects=True, vmem_limit_bytes=58 * 1024 * 1024
        ),
        cost_estimate=pl.CostEstimate(
            flops=2 * peers * rows * (depth + rank) * width,
            bytes_accessed=2 * (depth + rank) * width,
            transcendentals=0,
        ),
    )(attn, target.reshape(1, rows), target.reshape(rows, 1), down.T, weight, up)


def on_device(
    queries,
    token_key_rows,
    token_value_rows,
    stored_key_cache,
    stored_value_cache,
    cache_position_length,
    request_adapter_index,
    adapter_slot_index,
    output_projection_weight,
    down_factor_weight,
    up_factor_weight,
):
    attn = attend(
        queries,
        token_key_rows,
        token_value_rows,
        stored_key_cache,
        stored_value_cache,
        cache_position_length,
    )
    row_count = attn.shape[0]
    peers = lax.axis_size("tensor")
    adapter_count = adapter_slot_index.shape[0]
    home = jnp.sum(
        jnp.where(
            request_adapter_index == jnp.arange(adapter_count, dtype=jnp.int32)[None, :],
            adapter_slot_index[None, :],
            0,
        ),
        axis=1,
    )
    positions = jnp.arange(row_count, dtype=jnp.int32)
    same_home = (home[:, None] == home[None, :]) & (positions[:, None] > positions[None, :])
    rank_in_home = jnp.sum(same_home.astype(jnp.int32), axis=1)
    target = home * MOST + rank_in_home
    return project_and_sum(
        attn,
        target,
        down_factor_weight[0],
        output_projection_weight,
        up_factor_weight[0],
        peers,
    )


def solution(mesh):
    in_specs = (
        P(("groups", "dp", "tensor"), None),
        P(("groups", "dp", "tensor"), None),
        P(("groups", "dp", "tensor"), None),
        P(("groups", "dp", "tensor"), None, None),
        P(("groups", "dp", "tensor"), None, None),
        P(("groups", "dp", "tensor")),
        P(("groups", "dp", "tensor"), None),
        P(),
        P("tensor", None),
        P("tensor", None, None),
        P("tensor", None, None),
    )
    out_specs = P(("groups", "dp", "tensor"), None)
    return jax.shard_map(
        on_device, mesh=mesh, in_specs=in_specs, out_specs=out_specs, check_vma=False
    )
```

```python
import functools

import jax
import jax.numpy as jnp
from jax import lax
from jax.experimental import pallas as pl
from jax.experimental.pallas import tpu as pltpu
from jax.sharding import PartitionSpec as P

H = 32
KVH = 4
HD = 128
MOST = 4


def attend(
    queries,
    token_key_rows,
    token_value_rows,
    stored_key_cache,
    stored_value_cache,
    cache_position_length,
):
    req_count = queries.shape[0]
    cache_len = stored_key_cache.shape[1]
    per_group = H // KVH
    score_scale = HD ** (-0.5)
    query_heads = queries.reshape(req_count, KVH, per_group, HD)
    cached_keys = stored_key_cache.reshape(req_count, cache_len, KVH, HD)
    cached_values = stored_value_cache.reshape(req_count, cache_len, KVH, HD)
    fresh_keys = token_key_rows.reshape(req_count, KVH, HD)
    fresh_values = token_value_rows.astype(jnp.float32).reshape(req_count, KVH, HD)
    scores = (
        jnp.einsum("rkgd,rlkd->rkgl", query_heads, cached_keys, preferred_element_type=jnp.float32)
        * score_scale
    )
    fresh = (
        jnp.einsum("rkgd,rkd->rkg", query_heads, fresh_keys, preferred_element_type=jnp.float32)
        * score_scale
    )
    live = (jnp.arange(cache_len, dtype=jnp.int32)[None, :] < cache_position_length[:, None])[
        :, None, None, :
    ]
    row_top = jnp.maximum(jnp.max(jnp.where(live, scores, -1e30), axis=-1), fresh)
    weights = jnp.where(live, jnp.exp(scores - row_top[..., None]), 0.0)
    fresh_weight = jnp.exp(fresh - row_top)
    total = jnp.sum(weights, axis=-1) + fresh_weight
    probs = (weights / total[..., None]).astype(jnp.bfloat16)
    fresh_prob = (fresh_weight / total).astype(jnp.bfloat16)
    summed = jnp.einsum("rkgl,rlkd->rkgd", probs, cached_values, preferred_element_type=jnp.float32)
    summed = summed + fresh_prob.astype(jnp.float32)[..., None] * fresh_values[:, :, None, :]
    return summed.reshape(req_count, KVH * per_group * HD).astype(jnp.bfloat16)


CHUNKS = 16


def project_kernel(
    lines,
    attn_ref,
    target_row_ref,
    down_ref,
    weight_ref,
    up_ref,
    out_ref,
    row_outbox,
    row_inbox,
    outbox,
    inbox,
    lhs_ref,
    weights,
    pair_out,
    pair_in,
    line_out,
    line_in,
    own,
    kept,
    mail_send,
    mail_recv,
    weight_sem,
    up_sem,
    pair_send,
    pair_recv,
    line_send,
    line_recv,
):
    me = lax.axis_index("tensor")
    line, side = me // 2, me % 2
    other = 2 * line + (1 - side)
    depth = weight_ref.shape[0]
    rank = up_ref.shape[0]
    rows = lhs_ref.shape[2]
    span = pair_out.shape[3]
    peers = 2 * lines
    blocks = rows // MOST
    block = attn_ref.shape[1] // blocks

    def columns(c):
        return pl.ds(pl.multiple_of(c * span, span), span)

    def weight_copy(c):
        return pltpu.make_async_copy(
            weight_ref.at[:, columns(c)], weights.at[c, pl.ds(0, depth)], weight_sem.at[c]
        )

    def up_copy(c):
        return pltpu.make_async_copy(
            up_ref.at[:, columns(c)], weights.at[c, pl.ds(depth, rank)], up_sem.at[c]
        )

    def mail_copy(kind, k):
        to = (me + k) % peers
        outgoing, incoming = (row_outbox, row_inbox) if kind == 0 else (outbox, inbox)
        return pltpu.make_async_remote_copy(
            src_ref=outgoing.at[to],
            dst_ref=incoming.at[me],
            send_sem=mail_send.at[kind, k - 1],
            recv_sem=mail_recv.at[kind, k - 1],
            device_id={"tensor": to},
            device_id_type=pl.DeviceIdType.MESH,
        )

    def pair_copy(c):
        return pltpu.make_async_remote_copy(
            src_ref=pair_out.at[c],
            dst_ref=pair_in.at[c],
            send_sem=pair_send.at[c],
            recv_sem=pair_recv.at[c],
            device_id={"tensor": other},
            device_id_type=pl.DeviceIdType.MESH,
        )

    def line_copy(c, k):
        to = (line + k) % lines
        return pltpu.make_async_remote_copy(
            src_ref=line_out.at[c, k],
            dst_ref=line_in.at[c, k - 1],
            send_sem=line_send.at[c, k - 1],
            recv_sem=line_recv.at[c, k - 1],
            device_id={"tensor": 2 * to + side},
            device_id_type=pl.DeviceIdType.MESH,
        )

    @pl.loop(0, CHUNKS)
    def _(c):
        weight_copy(c).start()
        up_copy(c).start()

    barrier = pltpu.get_barrier_semaphore()
    for k in range(1, peers):
        pl.semaphore_signal(
            barrier,
            inc=1,
            device_id={"tensor": (me + k) % peers},
            device_id_type=pl.DeviceIdType.MESH,
        )

    picked_shape = (peers * rows, rows)
    spot = lax.broadcasted_iota(jnp.int32, picked_shape, 0)
    wanted = (spot // rows) * MOST + (spot % rows) // blocks
    match = wanted == jnp.broadcast_to(target_row_ref[...], picked_shape)
    picked = jnp.zeros((peers * rows, block), jnp.float32)
    for b in range(blocks):
        pick = jnp.where(match & (spot % blocks == b), 1.0, 0.0).astype(jnp.bfloat16)
        picked = picked + jnp.dot(
            pick,
            attn_ref[:, b * block : (b + 1) * block],
            preferred_element_type=jnp.float32,
        )
    row_outbox[:, :, :block] = picked.astype(jnp.bfloat16).reshape(peers, rows, block)
    diagonal = lax.broadcasted_iota(jnp.int32, (rows, rows), 0) == lax.broadcasted_iota(
        jnp.int32, (rows, rows), 1
    )
    target = jnp.where(diagonal, jnp.broadcast_to(target_row_ref[...], (rows, rows)), 0)
    target = jnp.broadcast_to(jnp.sum(target, axis=1, keepdims=True), (rows, 128))
    lane = lax.broadcasted_iota(jnp.int32, (rows, 128), 1)
    for p in range(peers):
        here = (target // MOST == p) & (lane == me * MOST + target % MOST)
        row_outbox[p, :, block:] = jnp.where(here, 1.0, 0.0).astype(jnp.bfloat16)
    pl.semaphore_wait(barrier, peers - 1)
    for k in range(1, peers):
        mail_copy(0, k).start()
    for p in range(peers):
        outbox[p] = attn_ref[:, p * depth : (p + 1) * depth]
    for k in range(1, peers):
        mail_copy(1, k).start()
    row_inbox[me] = row_outbox[me]
    inbox[me] = outbox[me]
    for k in range(1, peers):
        mail_copy(0, k).wait_recv()

    arrived = row_inbox[:, :, :block].reshape(peers * rows, block)
    spot = lax.broadcasted_iota(jnp.int32, (peers * rows, rank), 0)
    low = jnp.zeros((peers * rows, rank), jnp.float32)
    for b in range(blocks):
        term = lax.dot_general(
            arrived,
            down_ref[:, b * block : (b + 1) * block],
            (((1,), (1,)), ((), ())),
            preferred_element_type=jnp.float32,
        )
        low = low + jnp.where(spot % blocks == b, term, 0.0)
    low = jnp.sum(low.reshape(peers * MOST, blocks, rank), axis=1)
    low = jnp.concatenate([low, jnp.zeros((128 - peers * MOST, rank), jnp.float32)], axis=0)
    place = row_inbox[:, :, block:].reshape(peers * rows, 128)
    placed = jnp.dot(place, low.astype(jnp.bfloat16), preferred_element_type=jnp.float32)
    placed = placed.astype(jnp.bfloat16).reshape(lines, 2, rows, rank)
    lhs_ref[:, :, :, depth:] = placed
    for k in range(1, peers):
        mail_copy(1, k).wait_recv()
    lhs_ref[:, :, :, :depth] = inbox[...].reshape(lines, 2, rows, depth)

    @pl.loop(0, CHUNKS)
    def _(c):
        weight_copy(c).wait()
        up_copy(c).wait()
        left = lhs_ref[:, 1 - side].reshape(lines * rows, depth + rank)
        part = jnp.dot(left, weights[c], preferred_element_type=jnp.float32)
        pair_out[c] = part.astype(jnp.bfloat16).reshape(lines, rows, span)
        pair_copy(c).start()

    @pl.loop(0, CHUNKS)
    def _(c):
        left = lhs_ref[:, side].reshape(lines * rows, depth + rank)
        part = jnp.dot(left, weights[c], preferred_element_type=jnp.float32)
        pair_own = part.reshape(lines, rows, span)
        own[...] = pair_own
        pair_copy(c).wait_recv()
        for k in range(lines):
            to = (line + k) % lines
            both = own[to] + pair_in[c, to].astype(jnp.float32)
            if k == 0:
                kept[c] = both
            else:
                line_out[c, k] = both.astype(jnp.bfloat16)
                line_copy(c, k).start()

    @pl.loop(0, CHUNKS)
    def _(c):
        total = kept[c]
        for k in range(1, lines):
            line_copy(c, k).wait_recv()
            total = total + line_in[c, k - 1].astype(jnp.float32)
        out_ref[:, columns(c)] = total.astype(jnp.bfloat16)

    @pl.loop(0, CHUNKS)
    def _(c):
        pair_copy(c).wait_send()
        for k in range(1, lines):
            line_copy(c, k).wait_send()

    for k in range(1, peers):
        mail_copy(0, k).wait_send()
        mail_copy(1, k).wait_send()


def project_and_sum(attn, target, down, weight, up, peers):
    lines = peers // 2
    rows = attn.shape[0]
    depth, width = weight.shape
    rank = up.shape[0]
    span = width // CHUNKS
    letter = MOST * attn.shape[1] // rows + 128
    dma = pltpu.SemaphoreType.DMA
    return pl.pallas_call(
        functools.partial(project_kernel, lines),
        out_shape=jax.ShapeDtypeStruct((rows, width), jnp.bfloat16),
        in_specs=[
            pl.BlockSpec(memory_space=pltpu.VMEM),
            pl.BlockSpec(memory_space=pltpu.VMEM),
            pl.BlockSpec(memory_space=pltpu.VMEM),
            pl.BlockSpec(memory_space=pl.ANY),
            pl.BlockSpec(memory_space=pl.ANY),
        ],
        out_specs=pl.BlockSpec(memory_space=pltpu.VMEM),
        scratch_shapes=[
            pltpu.VMEM((peers, rows, letter), jnp.bfloat16),
            pltpu.VMEM((peers, rows, letter), jnp.bfloat16),
            pltpu.VMEM((peers, rows, depth), jnp.bfloat16),
            pltpu.VMEM((peers, rows, depth), jnp.bfloat16),
            pltpu.VMEM((lines, 2, rows, depth + rank), jnp.bfloat16),
            pltpu.VMEM((CHUNKS, depth + rank, span), jnp.bfloat16),
            pltpu.VMEM((CHUNKS, lines, rows, span), jnp.bfloat16),
            pltpu.VMEM((CHUNKS, lines, rows, span), jnp.bfloat16),
            pltpu.VMEM((CHUNKS, lines, rows, span), jnp.bfloat16),
            pltpu.VMEM((CHUNKS, lines - 1, rows, span), jnp.bfloat16),
            pltpu.VMEM((lines, rows, span), jnp.float32),
            pltpu.VMEM((CHUNKS, rows, span), jnp.float32),
            dma((2, peers - 1)),
            dma((2, peers - 1)),
            dma((CHUNKS,)),
            dma((CHUNKS,)),
            dma((CHUNKS,)),
            dma((CHUNKS,)),
            dma((CHUNKS, lines - 1)),
            dma((CHUNKS, lines - 1)),
        ],
        compiler_params=pltpu.CompilerParams(
            collective_id=0, has_side_effects=True, vmem_limit_bytes=58 * 1024 * 1024
        ),
        cost_estimate=pl.CostEstimate(
            flops=2 * peers * rows * (depth + rank) * width,
            bytes_accessed=2 * (depth + rank) * width,
            transcendentals=0,
        ),
    )(attn, target.reshape(1, rows), down.T, weight, up)


def on_device(
    queries,
    token_key_rows,
    token_value_rows,
    stored_key_cache,
    stored_value_cache,
    cache_position_length,
    request_adapter_index,
    adapter_slot_index,
    output_projection_weight,
    down_factor_weight,
    up_factor_weight,
):
    attn = attend(
        queries,
        token_key_rows,
        token_value_rows,
        stored_key_cache,
        stored_value_cache,
        cache_position_length,
    )
    row_count = attn.shape[0]
    peers = lax.axis_size("tensor")
    adapter_count = adapter_slot_index.shape[0]
    home = jnp.sum(
        jnp.where(
            request_adapter_index == jnp.arange(adapter_count, dtype=jnp.int32)[None, :],
            adapter_slot_index[None, :],
            0,
        ),
        axis=1,
    )
    positions = jnp.arange(row_count, dtype=jnp.int32)
    same_home = (home[:, None] == home[None, :]) & (positions[:, None] > positions[None, :])
    rank_in_home = jnp.sum(same_home.astype(jnp.int32), axis=1)
    target = home * MOST + rank_in_home
    return project_and_sum(
        attn,
        target,
        down_factor_weight[0],
        output_projection_weight,
        up_factor_weight[0],
        peers,
    )


def solution(mesh):
    in_specs = (
        P(("groups", "dp", "tensor"), None),
        P(("groups", "dp", "tensor"), None),
        P(("groups", "dp", "tensor"), None),
        P(("groups", "dp", "tensor"), None, None),
        P(("groups", "dp", "tensor"), None, None),
        P(("groups", "dp", "tensor")),
        P(("groups", "dp", "tensor"), None),
        P(),
        P("tensor", None),
        P("tensor", None, None),
        P("tensor", None, None),
    )
    out_specs = P(("groups", "dp", "tensor"), None)
    return jax.shard_map(
        on_device, mesh=mesh, in_specs=in_specs, out_specs=out_specs, check_vma=False
    )
```

```python
import functools

import jax
import jax.numpy as jnp
from jax import lax
from jax.experimental import pallas as pl
from jax.experimental.pallas import tpu as pltpu
from jax.sharding import PartitionSpec as P

H = 32
KVH = 4
HD = 128
MOST = 4


def attend(
    queries,
    token_key_rows,
    token_value_rows,
    stored_key_cache,
    stored_value_cache,
    cache_position_length,
):
    req_count = queries.shape[0]
    cache_len = stored_key_cache.shape[1]
    per_group = H // KVH
    score_scale = HD ** (-0.5)
    query_heads = queries.reshape(req_count, KVH, per_group, HD)
    cached_keys = stored_key_cache.reshape(req_count, cache_len, KVH, HD)
    cached_values = stored_value_cache.reshape(req_count, cache_len, KVH, HD)
    fresh_keys = token_key_rows.reshape(req_count, KVH, HD)
    fresh_values = token_value_rows.astype(jnp.float32).reshape(req_count, KVH, HD)
    scores = (
        jnp.einsum("rkgd,rlkd->rkgl", query_heads, cached_keys, preferred_element_type=jnp.float32)
        * score_scale
    )
    fresh = (
        jnp.einsum("rkgd,rkd->rkg", query_heads, fresh_keys, preferred_element_type=jnp.float32)
        * score_scale
    )
    live = (jnp.arange(cache_len, dtype=jnp.int32)[None, :] < cache_position_length[:, None])[
        :, None, None, :
    ]
    row_top = jnp.maximum(jnp.max(jnp.where(live, scores, -1e30), axis=-1), fresh)
    weights = jnp.where(live, jnp.exp(scores - row_top[..., None]), 0.0)
    fresh_weight = jnp.exp(fresh - row_top)
    total = jnp.sum(weights, axis=-1) + fresh_weight
    probs = (weights / total[..., None]).astype(jnp.bfloat16)
    fresh_prob = (fresh_weight / total).astype(jnp.bfloat16)
    summed = jnp.einsum("rkgl,rlkd->rkgd", probs, cached_values, preferred_element_type=jnp.float32)
    summed = summed + fresh_prob.astype(jnp.float32)[..., None] * fresh_values[:, :, None, :]
    return summed.reshape(req_count, KVH * per_group * HD).astype(jnp.bfloat16)


CHUNKS = 16


def project_kernel(
    lines,
    attn_ref,
    target_row_ref,
    down_ref,
    weight_ref,
    up_ref,
    out_ref,
    row_outbox,
    row_inbox,
    outbox,
    inbox,
    lhs_ref,
    weights,
    pair_out,
    pair_in,
    near_out,
    near_in,
    line_out,
    line_in,
    own,
    kept,
    mail_send,
    mail_recv,
    weight_sem,
    up_sem,
    pair_send,
    pair_recv,
    near_send,
    near_recv,
    line_send,
    line_recv,
):
    me = lax.axis_index("tensor")
    line, side = me // 2, me % 2
    half, parity = line // 2, line % 2
    halves = lines // 2
    other = 2 * line + (1 - side)
    depth = weight_ref.shape[0]
    rank = up_ref.shape[0]
    rows = lhs_ref.shape[2]
    span = pair_out.shape[3]
    peers = 2 * lines
    blocks = rows // MOST
    block = attn_ref.shape[1] // blocks

    def columns(c):
        return pl.ds(pl.multiple_of(c * span, span), span)

    def weight_copy(c):
        return pltpu.make_async_copy(
            weight_ref.at[:, columns(c)], weights.at[c, pl.ds(0, depth)], weight_sem.at[c]
        )

    def up_copy(c):
        return pltpu.make_async_copy(
            up_ref.at[:, columns(c)], weights.at[c, pl.ds(depth, rank)], up_sem.at[c]
        )

    def mail_copy(kind, k):
        to = (me + k) % peers
        outgoing, incoming = (row_outbox, row_inbox) if kind == 0 else (outbox, inbox)
        return pltpu.make_async_remote_copy(
            src_ref=outgoing.at[to],
            dst_ref=incoming.at[me],
            send_sem=mail_send.at[kind, k - 1],
            recv_sem=mail_recv.at[kind, k - 1],
            device_id={"tensor": to},
            device_id_type=pl.DeviceIdType.MESH,
        )

    def pair_copy(c):
        return pltpu.make_async_remote_copy(
            src_ref=pair_out.at[c],
            dst_ref=pair_in.at[c],
            send_sem=pair_send.at[c],
            recv_sem=pair_recv.at[c],
            device_id={"tensor": other},
            device_id_type=pl.DeviceIdType.MESH,
        )

    def near_copy(c):
        return pltpu.make_async_remote_copy(
            src_ref=near_out.at[c],
            dst_ref=near_in.at[c],
            send_sem=near_send.at[c],
            recv_sem=near_recv.at[c],
            device_id={"tensor": 2 * (2 * half + 1 - parity) + side},
            device_id_type=pl.DeviceIdType.MESH,
        )

    def line_copy(c, k):
        to = 2 * ((half + k) % halves) + parity
        return pltpu.make_async_remote_copy(
            src_ref=line_out.at[c, k - 1],
            dst_ref=line_in.at[c, k - 1],
            send_sem=line_send.at[c, k - 1],
            recv_sem=line_recv.at[c, k - 1],
            device_id={"tensor": 2 * to + side},
            device_id_type=pl.DeviceIdType.MESH,
        )

    @pl.loop(0, CHUNKS)
    def _(c):
        weight_copy(c).start()
        up_copy(c).start()

    barrier = pltpu.get_barrier_semaphore()
    for k in range(1, peers):
        pl.semaphore_signal(
            barrier,
            inc=1,
            device_id={"tensor": (me + k) % peers},
            device_id_type=pl.DeviceIdType.MESH,
        )

    picked_shape = (peers * rows, rows)
    spot = lax.broadcasted_iota(jnp.int32, picked_shape, 0)
    wanted = (spot // rows) * MOST + (spot % rows) // blocks
    match = wanted == jnp.broadcast_to(target_row_ref[...], picked_shape)
    picked = jnp.zeros((peers * rows, block), jnp.float32)
    for b in range(blocks):
        pick = jnp.where(match & (spot % blocks == b), 1.0, 0.0).astype(jnp.bfloat16)
        picked = picked + jnp.dot(
            pick,
            attn_ref[:, b * block : (b + 1) * block],
            preferred_element_type=jnp.float32,
        )
    row_outbox[:, :, :block] = picked.astype(jnp.bfloat16).reshape(peers, rows, block)
    diagonal = lax.broadcasted_iota(jnp.int32, (rows, rows), 0) == lax.broadcasted_iota(
        jnp.int32, (rows, rows), 1
    )
    target = jnp.where(diagonal, jnp.broadcast_to(target_row_ref[...], (rows, rows)), 0)
    target = jnp.broadcast_to(jnp.sum(target, axis=1, keepdims=True), (rows, 128))
    lane = lax.broadcasted_iota(jnp.int32, (rows, 128), 1)
    for p in range(peers):
        here = (target // MOST == p) & (lane == me * MOST + target % MOST)
        row_outbox[p, :, block:] = jnp.where(here, 1.0, 0.0).astype(jnp.bfloat16)
    pl.semaphore_wait(barrier, peers - 1)
    for k in range(1, peers):
        mail_copy(0, k).start()
    for p in range(peers):
        outbox[p] = attn_ref[:, p * depth : (p + 1) * depth]
    for k in range(1, peers):
        mail_copy(1, k).start()
    row_inbox[me] = row_outbox[me]
    inbox[me] = outbox[me]
    for k in range(1, peers):
        mail_copy(0, k).wait_recv()

    arrived = row_inbox[:, :, :block].reshape(peers * rows, block)
    spot = lax.broadcasted_iota(jnp.int32, (peers * rows, rank), 0)
    low = jnp.zeros((peers * rows, rank), jnp.float32)
    for b in range(blocks):
        term = lax.dot_general(
            arrived,
            down_ref[:, b * block : (b + 1) * block],
            (((1,), (1,)), ((), ())),
            preferred_element_type=jnp.float32,
        )
        low = low + jnp.where(spot % blocks == b, term, 0.0)
    low = jnp.sum(low.reshape(peers * MOST, blocks, rank), axis=1)
    low = jnp.concatenate([low, jnp.zeros((128 - peers * MOST, rank), jnp.float32)], axis=0)
    place = row_inbox[:, :, block:].reshape(peers * rows, 128)
    placed = jnp.dot(place, low.astype(jnp.bfloat16), preferred_element_type=jnp.float32)
    placed = placed.astype(jnp.bfloat16).reshape(lines, 2, rows, rank)
    lhs_ref[:, :, :, depth:] = placed
    for k in range(1, peers):
        mail_copy(1, k).wait_recv()
    lhs_ref[:, :, :, :depth] = inbox[...].reshape(lines, 2, rows, depth)

    @pl.loop(0, CHUNKS)
    def _(c):
        weight_copy(c).wait()
        up_copy(c).wait()
        left = lhs_ref[:, 1 - side].reshape(lines * rows, depth + rank)
        part = jnp.dot(left, weights[c], preferred_element_type=jnp.float32)
        pair_out[c] = part.astype(jnp.bfloat16).reshape(lines, rows, span)
        pair_copy(c).start()

    @pl.loop(0, CHUNKS)
    def _(c):
        left = lhs_ref[:, side].reshape(lines * rows, depth + rank)
        part = jnp.dot(left, weights[c], preferred_element_type=jnp.float32)
        pair_own = part.reshape(lines, rows, span)
        own[...] = pair_own
        pair_copy(c).wait_recv()
        for i in range(halves):
            to = 2 * i + 1 - parity
            both = own[to] + pair_in[c, to].astype(jnp.float32)
            near_out[c, i] = both.astype(jnp.bfloat16)
        near_copy(c).start()
        for i in range(halves):
            to = 2 * i + parity
            kept[c, i] = own[to] + pair_in[c, to].astype(jnp.float32)

    @pl.loop(0, CHUNKS)
    def _(c):
        near_copy(c).wait_recv()
        for k in range(1, halves):
            i = (half + k) % halves
            both = kept[c, i] + near_in[c, i].astype(jnp.float32)
            line_out[c, k - 1] = both.astype(jnp.bfloat16)
            line_copy(c, k).start()

    @pl.loop(0, CHUNKS)
    def _(c):
        total = kept[c, half] + near_in[c, half].astype(jnp.float32)
        for k in range(1, halves):
            line_copy(c, k).wait_recv()
            total = total + line_in[c, k - 1].astype(jnp.float32)
        out_ref[:, columns(c)] = total.astype(jnp.bfloat16)

    @pl.loop(0, CHUNKS)
    def _(c):
        pair_copy(c).wait_send()
        near_copy(c).wait_send()
        for k in range(1, halves):
            line_copy(c, k).wait_send()

    for k in range(1, peers):
        mail_copy(0, k).wait_send()
        mail_copy(1, k).wait_send()


def project_and_sum(attn, target, down, weight, up, peers):
    lines = peers // 2
    rows = attn.shape[0]
    depth, width = weight.shape
    rank = up.shape[0]
    span = width // CHUNKS
    letter = MOST * attn.shape[1] // rows + 128
    dma = pltpu.SemaphoreType.DMA
    return pl.pallas_call(
        functools.partial(project_kernel, lines),
        out_shape=jax.ShapeDtypeStruct((rows, width), jnp.bfloat16),
        in_specs=[
            pl.BlockSpec(memory_space=pltpu.VMEM),
            pl.BlockSpec(memory_space=pltpu.VMEM),
            pl.BlockSpec(memory_space=pltpu.VMEM),
            pl.BlockSpec(memory_space=pl.ANY),
            pl.BlockSpec(memory_space=pl.ANY),
        ],
        out_specs=pl.BlockSpec(memory_space=pltpu.VMEM),
        scratch_shapes=[
            pltpu.VMEM((peers, rows, letter), jnp.bfloat16),
            pltpu.VMEM((peers, rows, letter), jnp.bfloat16),
            pltpu.VMEM((peers, rows, depth), jnp.bfloat16),
            pltpu.VMEM((peers, rows, depth), jnp.bfloat16),
            pltpu.VMEM((lines, 2, rows, depth + rank), jnp.bfloat16),
            pltpu.VMEM((CHUNKS, depth + rank, span), jnp.bfloat16),
            pltpu.VMEM((CHUNKS, lines, rows, span), jnp.bfloat16),
            pltpu.VMEM((CHUNKS, lines, rows, span), jnp.bfloat16),
            pltpu.VMEM((CHUNKS, lines // 2, rows, span), jnp.bfloat16),
            pltpu.VMEM((CHUNKS, lines // 2, rows, span), jnp.bfloat16),
            pltpu.VMEM((CHUNKS, lines // 2 - 1, rows, span), jnp.bfloat16),
            pltpu.VMEM((CHUNKS, lines // 2 - 1, rows, span), jnp.bfloat16),
            pltpu.VMEM((lines, rows, span), jnp.float32),
            pltpu.VMEM((CHUNKS, lines // 2, rows, span), jnp.float32),
            dma((2, peers - 1)),
            dma((2, peers - 1)),
            dma((CHUNKS,)),
            dma((CHUNKS,)),
            dma((CHUNKS,)),
            dma((CHUNKS,)),
            dma((CHUNKS,)),
            dma((CHUNKS,)),
            dma((CHUNKS, lines // 2 - 1)),
            dma((CHUNKS, lines // 2 - 1)),
        ],
        compiler_params=pltpu.CompilerParams(
            collective_id=0, has_side_effects=True, vmem_limit_bytes=58 * 1024 * 1024
        ),
        cost_estimate=pl.CostEstimate(
            flops=2 * peers * rows * (depth + rank) * width,
            bytes_accessed=2 * (depth + rank) * width,
            transcendentals=0,
        ),
    )(attn, target.reshape(1, rows), down.T, weight, up)


def on_device(
    queries,
    token_key_rows,
    token_value_rows,
    stored_key_cache,
    stored_value_cache,
    cache_position_length,
    request_adapter_index,
    adapter_slot_index,
    output_projection_weight,
    down_factor_weight,
    up_factor_weight,
):
    attn = attend(
        queries,
        token_key_rows,
        token_value_rows,
        stored_key_cache,
        stored_value_cache,
        cache_position_length,
    )
    row_count = attn.shape[0]
    peers = lax.axis_size("tensor")
    adapter_count = adapter_slot_index.shape[0]
    home = jnp.sum(
        jnp.where(
            request_adapter_index == jnp.arange(adapter_count, dtype=jnp.int32)[None, :],
            adapter_slot_index[None, :],
            0,
        ),
        axis=1,
    )
    positions = jnp.arange(row_count, dtype=jnp.int32)
    same_home = (home[:, None] == home[None, :]) & (positions[:, None] > positions[None, :])
    rank_in_home = jnp.sum(same_home.astype(jnp.int32), axis=1)
    target = home * MOST + rank_in_home
    return project_and_sum(
        attn,
        target,
        down_factor_weight[0],
        output_projection_weight,
        up_factor_weight[0],
        peers,
    )


def solution(mesh):
    in_specs = (
        P(("groups", "dp", "tensor"), None),
        P(("groups", "dp", "tensor"), None),
        P(("groups", "dp", "tensor"), None),
        P(("groups", "dp", "tensor"), None, None),
        P(("groups", "dp", "tensor"), None, None),
        P(("groups", "dp", "tensor")),
        P(("groups", "dp", "tensor"), None),
        P(),
        P("tensor", None),
        P("tensor", None, None),
        P("tensor", None, None),
    )
    out_specs = P(("groups", "dp", "tensor"), None)
    return jax.shard_map(
        on_device, mesh=mesh, in_specs=in_specs, out_specs=out_specs, check_vma=False
    )
```

```python
import functools

import jax
import jax.numpy as jnp
from jax import lax
from jax.experimental import pallas as pl
from jax.experimental.pallas import tpu as pltpu
from jax.sharding import PartitionSpec as P

H = 32
KVH = 4
HD = 128
MOST = 4


def attend(
    queries,
    token_key_rows,
    token_value_rows,
    stored_key_cache,
    stored_value_cache,
    cache_position_length,
):
    req_count = queries.shape[0]
    cache_len = stored_key_cache.shape[1]
    per_group = H // KVH
    score_scale = HD ** (-0.5)
    query_heads = queries.reshape(req_count, KVH, per_group, HD)
    cached_keys = stored_key_cache.reshape(req_count, cache_len, KVH, HD)
    cached_values = stored_value_cache.reshape(req_count, cache_len, KVH, HD)
    fresh_keys = token_key_rows.reshape(req_count, KVH, HD)
    fresh_values = token_value_rows.astype(jnp.float32).reshape(req_count, KVH, HD)
    scores = (
        jnp.einsum("rkgd,rlkd->rkgl", query_heads, cached_keys, preferred_element_type=jnp.float32)
        * score_scale
    )
    fresh = (
        jnp.einsum("rkgd,rkd->rkg", query_heads, fresh_keys, preferred_element_type=jnp.float32)
        * score_scale
    )
    live = (jnp.arange(cache_len, dtype=jnp.int32)[None, :] < cache_position_length[:, None])[
        :, None, None, :
    ]
    row_top = jnp.maximum(jnp.max(jnp.where(live, scores, -1e30), axis=-1), fresh)
    weights = jnp.where(live, jnp.exp(scores - row_top[..., None]), 0.0)
    fresh_weight = jnp.exp(fresh - row_top)
    total = jnp.sum(weights, axis=-1) + fresh_weight
    probs = (weights / total[..., None]).astype(jnp.bfloat16)
    fresh_prob = (fresh_weight / total).astype(jnp.bfloat16)
    summed = jnp.einsum("rkgl,rlkd->rkgd", probs, cached_values, preferred_element_type=jnp.float32)
    summed = summed + fresh_prob.astype(jnp.float32)[..., None] * fresh_values[:, :, None, :]
    return summed.reshape(req_count, KVH * per_group * HD).astype(jnp.bfloat16)


CHUNKS = 16


def project_kernel(
    lines,
    attn_ref,
    target_row_ref,
    down_ref,
    weight_ref,
    up_ref,
    out_ref,
    row_outbox,
    row_inbox,
    outbox,
    inbox,
    lhs_ref,
    weights,
    pair_out,
    pair_in,
    near_out,
    near_in,
    line_out,
    line_in,
    own,
    kept,
    mail_send,
    mail_recv,
    weight_sem,
    up_sem,
    pair_send,
    pair_recv,
    near_send,
    near_recv,
    line_send,
    line_recv,
):
    me = lax.axis_index("tensor")
    line, side = me // 2, me % 2
    half, parity = line // 2, line % 2
    halves = lines // 2
    other = 2 * line + (1 - side)
    depth = weight_ref.shape[0]
    rank = up_ref.shape[0]
    rows = lhs_ref.shape[2]
    span = pair_out.shape[3]
    peers = 2 * lines
    blocks = rows // MOST
    block = attn_ref.shape[1] // blocks

    def columns(c):
        return pl.ds(pl.multiple_of(c * span, span), span)

    def weight_copy(c):
        return pltpu.make_async_copy(
            weight_ref.at[:, columns(c)], weights.at[c, pl.ds(0, depth)], weight_sem.at[c]
        )

    def up_copy(c):
        return pltpu.make_async_copy(
            up_ref.at[:, columns(c)], weights.at[c, pl.ds(depth, rank)], up_sem.at[c]
        )

    def mail_copy(kind, k):
        to = (me + k) % peers
        outgoing, incoming = (row_outbox, row_inbox) if kind == 0 else (outbox, inbox)
        return pltpu.make_async_remote_copy(
            src_ref=outgoing.at[to],
            dst_ref=incoming.at[me],
            send_sem=mail_send.at[kind, k - 1],
            recv_sem=mail_recv.at[kind, k - 1],
            device_id={"tensor": to},
            device_id_type=pl.DeviceIdType.MESH,
        )

    def pair_copy(c):
        return pltpu.make_async_remote_copy(
            src_ref=pair_out.at[c],
            dst_ref=pair_in.at[c],
            send_sem=pair_send.at[c],
            recv_sem=pair_recv.at[c],
            device_id={"tensor": other},
            device_id_type=pl.DeviceIdType.MESH,
        )

    def near_copy(c):
        return pltpu.make_async_remote_copy(
            src_ref=near_out.at[c],
            dst_ref=near_in.at[c],
            send_sem=near_send.at[c],
            recv_sem=near_recv.at[c],
            device_id={"tensor": 2 * (2 * half + 1 - parity) + side},
            device_id_type=pl.DeviceIdType.MESH,
        )

    def line_copy(c, k):
        to = 2 * ((half + k) % halves) + parity
        return pltpu.make_async_remote_copy(
            src_ref=line_out.at[c, k - 1],
            dst_ref=line_in.at[c, k - 1],
            send_sem=line_send.at[c, k - 1],
            recv_sem=line_recv.at[c, k - 1],
            device_id={"tensor": 2 * to + side},
            device_id_type=pl.DeviceIdType.MESH,
        )

    @pl.loop(0, CHUNKS)
    def _(c):
        weight_copy(c).start()
        up_copy(c).start()

    barrier = pltpu.get_barrier_semaphore()
    for k in range(1, peers):
        pl.semaphore_signal(
            barrier,
            inc=1,
            device_id={"tensor": (me + k) % peers},
            device_id_type=pl.DeviceIdType.MESH,
        )

    picked_shape = (peers * rows, rows)
    spot = lax.broadcasted_iota(jnp.int32, picked_shape, 0)
    wanted = (spot // rows) * MOST + (spot % rows) // blocks
    match = wanted == jnp.broadcast_to(target_row_ref[...], picked_shape)
    picked = jnp.zeros((peers * rows, block), jnp.float32)
    for b in range(blocks):
        pick = jnp.where(match & (spot % blocks == b), 1.0, 0.0).astype(jnp.bfloat16)
        picked = picked + jnp.dot(
            pick,
            attn_ref[:, b * block : (b + 1) * block],
            preferred_element_type=jnp.float32,
        )
    row_outbox[:, :, :block] = picked.astype(jnp.bfloat16).reshape(peers, rows, block)
    diagonal = lax.broadcasted_iota(jnp.int32, (rows, rows), 0) == lax.broadcasted_iota(
        jnp.int32, (rows, rows), 1
    )
    target = jnp.where(diagonal, jnp.broadcast_to(target_row_ref[...], (rows, rows)), 0)
    target = jnp.broadcast_to(jnp.sum(target, axis=1, keepdims=True), (rows, 128))
    lane = lax.broadcasted_iota(jnp.int32, (rows, 128), 1)
    for p in range(peers):
        here = (target // MOST == p) & (lane == me * MOST + target % MOST)
        row_outbox[p, :, block:] = jnp.where(here, 1.0, 0.0).astype(jnp.bfloat16)
    pl.semaphore_wait(barrier, peers - 1)
    for k in range(1, peers):
        mail_copy(0, k).start()
    for p in range(peers):
        outbox[p] = attn_ref[:, p * depth : (p + 1) * depth]
    for k in range(1, peers):
        mail_copy(1, k).start()
    row_inbox[me] = row_outbox[me]
    inbox[me] = outbox[me]
    for k in range(1, peers):
        mail_copy(0, k).wait_recv()

    arrived = row_inbox[:, :, :block].reshape(peers * rows, block)
    spot = lax.broadcasted_iota(jnp.int32, (peers * rows, rank), 0)
    low = jnp.zeros((peers * rows, rank), jnp.float32)
    for b in range(blocks):
        term = lax.dot_general(
            arrived,
            down_ref[:, b * block : (b + 1) * block],
            (((1,), (1,)), ((), ())),
            preferred_element_type=jnp.float32,
        )
        low = low + jnp.where(spot % blocks == b, term, 0.0)
    low = jnp.sum(low.reshape(peers * MOST, blocks, rank), axis=1)
    low = jnp.concatenate([low, jnp.zeros((128 - peers * MOST, rank), jnp.float32)], axis=0)
    place = row_inbox[:, :, block:].reshape(peers * rows, 128)
    placed = jnp.dot(place, low.astype(jnp.bfloat16), preferred_element_type=jnp.float32)
    placed = placed.astype(jnp.bfloat16).reshape(lines, 2, rows, rank)
    lhs_ref[:, :, :, depth:] = placed
    for k in range(1, peers):
        mail_copy(1, k).wait_recv()
    lhs_ref[:, :, :, :depth] = inbox[...].reshape(lines, 2, rows, depth)

    @pl.loop(0, CHUNKS)
    def _(c):
        weight_copy(c).wait()
        up_copy(c).wait()
        left = lhs_ref[:, 1 - side].reshape(lines * rows, depth + rank)
        part = jnp.dot(left, weights[c], preferred_element_type=jnp.float32)
        pair_out[c] = part.astype(jnp.bfloat16).reshape(lines, rows, span)
        pair_copy(c).start()

    def far_step(c):
        near_copy(c).wait_recv()
        for k in range(1, halves):
            i = (half + k) % halves
            both = kept[c, i] + near_in[c, i].astype(jnp.float32)
            line_out[c, k - 1] = both.astype(jnp.bfloat16)
            line_copy(c, k).start()

    @pl.loop(0, CHUNKS)
    def _(c):
        left = lhs_ref[:, side].reshape(lines * rows, depth + rank)
        part = jnp.dot(left, weights[c], preferred_element_type=jnp.float32)
        pair_own = part.reshape(lines, rows, span)
        own[...] = pair_own
        pair_copy(c).wait_recv()
        for i in range(halves):
            to = 2 * i + 1 - parity
            both = own[to] + pair_in[c, to].astype(jnp.float32)
            near_out[c, i] = both.astype(jnp.bfloat16)
        near_copy(c).start()
        for i in range(halves):
            to = 2 * i + parity
            kept[c, i] = own[to] + pair_in[c, to].astype(jnp.float32)

        @pl.when(c >= 2)
        def _():
            far_step(c - 2)

    far_step(CHUNKS - 2)
    far_step(CHUNKS - 1)

    @pl.loop(0, CHUNKS)
    def _(c):
        total = kept[c, half] + near_in[c, half].astype(jnp.float32)
        for k in range(1, halves):
            line_copy(c, k).wait_recv()
            total = total + line_in[c, k - 1].astype(jnp.float32)
        out_ref[:, columns(c)] = total.astype(jnp.bfloat16)

    @pl.loop(0, CHUNKS)
    def _(c):
        pair_copy(c).wait_send()
        near_copy(c).wait_send()
        for k in range(1, halves):
            line_copy(c, k).wait_send()

    for k in range(1, peers):
        mail_copy(0, k).wait_send()
        mail_copy(1, k).wait_send()


def project_and_sum(attn, target, down, weight, up, peers):
    lines = peers // 2
    rows = attn.shape[0]
    depth, width = weight.shape
    rank = up.shape[0]
    span = width // CHUNKS
    letter = MOST * attn.shape[1] // rows + 128
    dma = pltpu.SemaphoreType.DMA
    return pl.pallas_call(
        functools.partial(project_kernel, lines),
        out_shape=jax.ShapeDtypeStruct((rows, width), jnp.bfloat16),
        in_specs=[
            pl.BlockSpec(memory_space=pltpu.VMEM),
            pl.BlockSpec(memory_space=pltpu.VMEM),
            pl.BlockSpec(memory_space=pltpu.VMEM),
            pl.BlockSpec(memory_space=pl.ANY),
            pl.BlockSpec(memory_space=pl.ANY),
        ],
        out_specs=pl.BlockSpec(memory_space=pltpu.VMEM),
        scratch_shapes=[
            pltpu.VMEM((peers, rows, letter), jnp.bfloat16),
            pltpu.VMEM((peers, rows, letter), jnp.bfloat16),
            pltpu.VMEM((peers, rows, depth), jnp.bfloat16),
            pltpu.VMEM((peers, rows, depth), jnp.bfloat16),
            pltpu.VMEM((lines, 2, rows, depth + rank), jnp.bfloat16),
            pltpu.VMEM((CHUNKS, depth + rank, span), jnp.bfloat16),
            pltpu.VMEM((CHUNKS, lines, rows, span), jnp.bfloat16),
            pltpu.VMEM((CHUNKS, lines, rows, span), jnp.bfloat16),
            pltpu.VMEM((CHUNKS, lines // 2, rows, span), jnp.bfloat16),
            pltpu.VMEM((CHUNKS, lines // 2, rows, span), jnp.bfloat16),
            pltpu.VMEM((CHUNKS, lines // 2 - 1, rows, span), jnp.bfloat16),
            pltpu.VMEM((CHUNKS, lines // 2 - 1, rows, span), jnp.bfloat16),
            pltpu.VMEM((lines, rows, span), jnp.float32),
            pltpu.VMEM((CHUNKS, lines // 2, rows, span), jnp.float32),
            dma((2, peers - 1)),
            dma((2, peers - 1)),
            dma((CHUNKS,)),
            dma((CHUNKS,)),
            dma((CHUNKS,)),
            dma((CHUNKS,)),
            dma((CHUNKS,)),
            dma((CHUNKS,)),
            dma((CHUNKS, lines // 2 - 1)),
            dma((CHUNKS, lines // 2 - 1)),
        ],
        compiler_params=pltpu.CompilerParams(
            collective_id=0, has_side_effects=True, vmem_limit_bytes=58 * 1024 * 1024
        ),
        cost_estimate=pl.CostEstimate(
            flops=2 * peers * rows * (depth + rank) * width,
            bytes_accessed=2 * (depth + rank) * width,
            transcendentals=0,
        ),
    )(attn, target.reshape(1, rows), down.T, weight, up)


def on_device(
    queries,
    token_key_rows,
    token_value_rows,
    stored_key_cache,
    stored_value_cache,
    cache_position_length,
    request_adapter_index,
    adapter_slot_index,
    output_projection_weight,
    down_factor_weight,
    up_factor_weight,
):
    attn = attend(
        queries,
        token_key_rows,
        token_value_rows,
        stored_key_cache,
        stored_value_cache,
        cache_position_length,
    )
    row_count = attn.shape[0]
    peers = lax.axis_size("tensor")
    adapter_count = adapter_slot_index.shape[0]
    home = jnp.sum(
        jnp.where(
            request_adapter_index == jnp.arange(adapter_count, dtype=jnp.int32)[None, :],
            adapter_slot_index[None, :],
            0,
        ),
        axis=1,
    )
    positions = jnp.arange(row_count, dtype=jnp.int32)
    same_home = (home[:, None] == home[None, :]) & (positions[:, None] > positions[None, :])
    rank_in_home = jnp.sum(same_home.astype(jnp.int32), axis=1)
    target = home * MOST + rank_in_home
    return project_and_sum(
        attn,
        target,
        down_factor_weight[0],
        output_projection_weight,
        up_factor_weight[0],
        peers,
    )


def solution(mesh):
    in_specs = (
        P(("groups", "dp", "tensor"), None),
        P(("groups", "dp", "tensor"), None),
        P(("groups", "dp", "tensor"), None),
        P(("groups", "dp", "tensor"), None, None),
        P(("groups", "dp", "tensor"), None, None),
        P(("groups", "dp", "tensor")),
        P(("groups", "dp", "tensor"), None),
        P(),
        P("tensor", None),
        P("tensor", None, None),
        P("tensor", None, None),
    )
    out_specs = P(("groups", "dp", "tensor"), None)
    return jax.shard_map(
        on_device, mesh=mesh, in_specs=in_specs, out_specs=out_specs, check_vma=False
    )
```
